32 devices in a mesh: shard: 4 (over y, core), replica: 8 (over z, x).
Axes of the slice: x: 2, y: 2, z: 4, core: 2. Of those that a mesh axis runs over, the one named last changes fastest.
Arguments:
- tokens: bfloat16 [64, 256, 384], P(('shard', 'replica')), may hold values from -6 to 6
- condition: bfloat16 [64, 384], P(('shard', 'replica')), may hold values from -6 to 6
- cotangent: bfloat16 [64, 256, 384], P(('shard', 'replica')), may hold values from -6 to 6
- w_rows: bfloat16 [384, 5376], P('shard'), may hold values from -1.2247449 to 1.2247449
- w_down: bfloat16 [1536, 384], P('shard'), may hold values from -0.15625 to 0.15625
- bias_pack: bfloat16 [5376], P('shard'), may hold values from -1 to 1
- rows_first: bfloat16 [384, 5376], P('shard'), may hold values from -40.96 to 40.96
- rows_second: bfloat16 [384, 5376], P('shard'), may hold values from 0.32768 to 32.768
- down_first: bfloat16 [1536, 384], P('shard'), may hold values from -16.625 to 16.625
- down_second: bfloat16 [1536, 384], P('shard'), may hold values from 1.46875 to 5.875
- bias_first: bfloat16 [5376], P('shard'), may hold values from -69.12 to 69.12
- bias_second: bfloat16 [5376], P('shard'), may hold values from 0.32768 to 95.0272
Outputs:
- block_out: bfloat16 [64, 256, 384], P(('shard', 'replica'))
- tokens_grad: bfloat16 [64, 256, 384], P(('shard', 'replica'))
- cond_grad: float32 [64, 384], P(('shard', 'replica'))
- rows_new: float32 [384, 5376], P('shard')
- rows_first_new: float32 [384, 5376], P('shard')
- rows_second_new: float32 [384, 5376], P('shard')
- down_new: float32 [1536, 384], P('shard')
- down_first_new: float32 [1536, 384], P('shard')
- down_second_new: float32 [1536, 384], P('shard')
- bias_new: float32 [5376], P('shard')
- bias_first_new: float32 [5376], P('shard')
- bias_second_new: float32 [5376], P('shard')
The draws below stay inside these ranges and needn't reach their ends.
All inputs are finite; a program needn't handle non-finite values.
Results may differ from the reference program's by a relative error of at most 0.012.
The reference program's roundings to bfloat16 on the way count: a program that leaves them out, or rounds other values in their place, can miss the bound.
Values may be sent and summed in bfloat16 or wider, within the bound.
A program may use at most 128 MiB of HBM per device.

```python
import math
import jax
import jax.numpy as jnp
from jax import lax

D = 384
HEADS = 6
HEAD = 64
FF = 1536
SEQ = 256
STEP = 10
LAT = 64
TOKENS = 16384
PACK = 5376


def draw_w_rows(key, part):
    key = jax.random.fold_in(key, 11)
    entries = jax.random.normal(key, (D, 10 * D + FF), jnp.float32)
    column = lax.broadcasted_iota(jnp.int32, (D, 10 * D + FF), 1)
    widened = jnp.where((column >= 9 * D) & (column < 10 * D), 4.0, 1.0)
    return (jnp.clip(entries, -6.0, 6.0) * widened * D ** (-0.5)).astype(jnp.bfloat16)


def column_scale(shape):
    column = lax.broadcasted_iota(jnp.int32, shape, len(shape) - 1)
    scale = jnp.where(column < 6 * D, 0.7, 0.4)
    scale = jnp.where((column >= 6 * D) & (column < 9 * D), 0.15, scale)
    scale = jnp.where((column >= 9 * D) & (column < 10 * D), 0.25, scale)
    return scale


def bias_scale(shape):
    entry = lax.broadcasted_iota(jnp.int32, shape, 0)
    scale = jnp.where(entry < 6 * D, 1.2, 0.6)
    scale = jnp.where((entry >= 6 * D) & (entry < 8 * D), 0.15, scale)
    scale = jnp.where((entry >= 9 * D) & (entry < 9 * D + FF), 0.3, scale)
    return scale


def first_from(key, scale):
    entries = jnp.clip(jax.random.normal(key, scale.shape, jnp.float32), -4.0, 4.0)
    return (entries * 0.111 * scale * TOKENS ** 0.5).astype(jnp.bfloat16)


def second_from(key, scale):
    factor = jnp.exp(jax.random.uniform(key, scale.shape, jnp.float32, 0.0, 1.3862944))
    return (factor * 0.001 * scale * scale * TOKENS).astype(jnp.bfloat16)


def draw_rows_first(key, part):
    key = jax.random.fold_in(key, 21)
    return first_from(key, column_scale((D, 10 * D + FF)))


def draw_rows_second(key, part):
    key = jax.random.fold_in(key, 22)
    return second_from(key, column_scale((D, 10 * D + FF)))


def draw_bias_first(key, part):
    key = jax.random.fold_in(key, 23)
    return first_from(key, bias_scale((10 * D + FF,)))


def draw_bias_second(key, part):
    key = jax.random.fold_in(key, 24)
    return second_from(key, bias_scale((10 * D + FF,)))


def shard_levels(key, extent, split, least, high):
    def one(axis_at, parts):
        heights = jax.random.uniform(jax.random.fold_in(jax.random.fold_in(key, 6), axis_at), (parts,), jnp.float32, least / len(split), high / len(split))
        return jnp.repeat(jnp.exp(heights), extent[axis_at] // parts).reshape((-1,) + (1,) * (len(extent) - axis_at - 1))

    factor_of = one(*split[0])
    for cut in split[1:]:
        factor_of = factor_of * one(*cut)
    return factor_of


def noise(own_key, extent, spread, reach, cuts=(), dtype=jnp.bfloat16):
    loudness = shard_levels(own_key, extent, cuts, -0.22, 0.18) if cuts else 1.0
    values = jax.random.normal(own_key, extent, jnp.float32) * spread * loudness
    return jnp.minimum(jnp.maximum(values, -reach), reach).astype(dtype)


def setup_inputs(seed: int = 0) -> dict:
    streams_of = jax.random.split(jax.random.key(seed), 13)
    return {
        "tokens": noise(streams_of[0], (LAT, SEQ, D), 1.0, 6.0, ((0, 32),)),
        "condition": noise(streams_of[1], (LAT, D), 1.0, 6.0, ((0, 32),)),
        "cotangent": noise(streams_of[2], (LAT, SEQ, D), 1.0, 6.0, ((0, 32),)),
        "w_rows": draw_w_rows(jax.random.fold_in(streams_of[12], 71), 0),
        "w_down": noise(streams_of[4], (FF, D), FF ** -0.5, 0.15625, ((0, 4),)),
        "bias_pack": noise(streams_of[5], (PACK,), 0.2, 1.0, ((0, 4),)),
        "rows_first": draw_rows_first(jax.random.fold_in(streams_of[12], 71), 0),
        "rows_second": draw_rows_second(jax.random.fold_in(streams_of[12], 71), 0),
        "down_first": noise(streams_of[8], (FF, D), (0.033 * TOKENS ** 0.5), 16.625, ((0, 4),)),
        "down_second": jnp.clip(jnp.exp(math.log(5.875) - 1.3862944 * jax.random.uniform(streams_of[9], (FF, D), jnp.float32) ** shard_levels(streams_of[9], (FF, D), ((0, 4),), -0.2, 0.2)), 1.46875, 5.875).astype(jnp.bfloat16),
        "bias_first": draw_bias_first(jax.random.fold_in(streams_of[12], 71), 0),
        "bias_second": draw_bias_second(jax.random.fold_in(streams_of[12], 71), 0),
    }


@jax.custom_vjp
def low(v):
    return lax.optimization_barrier(v.astype(jnp.bfloat16)).astype(jnp.float32)

@jax.custom_vjp
def low_back(v):
    return v

def low_keep(v):
    return (low(v), None)

def low_pass(kept, grad):
    return (grad,)

def back_keep(v):
    return (v, None)

def back_low(kept, grad):
    return (low(grad),)
low.defvjp(low_keep, low_pass)
low_back.defvjp(back_keep, back_low)
norm_eps = 1e-06
beta_one = 0.9
beta_two = 0.999
adam_eps = 1e-08
decay_rate = 0.1
learn_rate = 0.1
highest = lax.Precision.HIGHEST

def product(spec_text, left, right):
    return jnp.einsum(spec_text, left, right, precision=highest, preferred_element_type=jnp.float32)

def normalize(values):
    average = lax.optimization_barrier(jnp.mean(values, axis=-1, keepdims=True))
    centered = values - average
    variance = lax.optimization_barrier(jnp.mean(centered * centered, axis=-1, keepdims=True))
    return centered * lax.rsqrt(variance + norm_eps)

def forward(w_rows, w_down, bias_pack, tokens, condition):
    groups = tokens.shape[0]
    silu_cond = low(jax.nn.silu(condition))
    modulation = low_back(product('gd,de->ge', silu_cond, w_rows[:, :6 * D]) + bias_pack[:6 * D])
    shift_attention = modulation[:, None, 0:D]
    scale_attention = modulation[:, None, D:2 * D]
    gate_attention = modulation[:, None, 2 * D:3 * D]
    shift_feed = modulation[:, None, 3 * D:4 * D]
    scale_feed = modulation[:, None, 4 * D:5 * D]
    gate_feed = modulation[:, None, 5 * D:6 * D]
    input_attention = low(normalize(tokens) * (1.0 + scale_attention) + shift_attention)
    projected = product('gsd,de->gse', input_attention, w_rows[:, 6 * D:9 * D])
    head_shape = (groups, SEQ, HEADS, HEAD)
    query = low_back(low(projected[..., :D] + bias_pack[6 * D:7 * D])).reshape(head_shape)
    keys = low_back(low(projected[..., D:2 * D])).reshape(head_shape)
    values = low_back(low(projected[..., 2 * D:] + bias_pack[7 * D:8 * D])).reshape(head_shape)
    scores = low_back(product('gqhe,gkhe->ghqk', query, keys) * HEAD ** (-0.5))
    weights = low(jax.nn.softmax(scores, axis=-1))
    mixed_heads = low_back(low(product('ghqk,gkhe->gqhe', weights, values).reshape(groups, SEQ, D)))
    branch = low_back(product('gsd,de->gse', mixed_heads, w_rows[:, 9 * D:10 * D]) + bias_pack[8 * D:9 * D])
    residual = tokens + gate_attention * branch
    feed_input = low(normalize(residual) * (1.0 + scale_feed) + shift_feed)
    hidden = low_back(product('gsd,df->gsf', feed_input, w_rows[:, 10 * D:]) + bias_pack[9 * D:9 * D + FF])
    activated_hidden = low(jax.nn.gelu(hidden, approximate=True))
    feed_out = low_back(product('gsf,fd->gsd', activated_hidden, w_down) + bias_pack[9 * D + FF:])
    return residual + gate_feed * feed_out

def adam_step(weight, gradient, moment_one, moment_two, weight_decay):
    first_new = beta_one * moment_one.astype(jnp.float32) + (1.0 - beta_one) * gradient
    second_new = beta_two * moment_two.astype(jnp.float32) + (1.0 - beta_two) * gradient * gradient
    first_hat = first_new / (1.0 - beta_one ** STEP)
    second_hat = second_new / (1.0 - beta_two ** STEP)
    master = weight.astype(jnp.float32)
    updated = master - learn_rate * (first_hat / (jnp.sqrt(second_hat) + adam_eps) + weight_decay * master)
    return (updated, first_new, second_new)

def reference(tokens, condition, cotangent, w_rows, w_down, bias_pack, rows_first, rows_second, down_first, down_second, bias_first, bias_second):
    per_scan = 16
    scan_steps = tokens.shape[0] // per_scan
    parameters = (w_rows.astype(jnp.float32), w_down.astype(jnp.float32), bias_pack.astype(jnp.float32))
    token_groups = tokens.astype(jnp.float32).reshape(scan_steps, per_scan, SEQ, D)
    cond_groups = condition.astype(jnp.float32).reshape(scan_steps, per_scan, D)
    upstream_groups = cotangent.astype(jnp.float32).reshape(scan_steps, per_scan, SEQ, D)

    def one_group(running, pieces):
        token_part, cond_part, upstream_part = pieces
        result, pullback = jax.vjp(forward, parameters[0], parameters[1], parameters[2], token_part, cond_part)
        gradients = pullback(upstream_part)
        running = (running[0] + gradients[0], running[1] + gradients[1], running[2] + gradients[2])
        return (running, (result, gradients[3], gradients[4]))
    initial = (jnp.zeros_like(parameters[0]), jnp.zeros_like(parameters[1]), jnp.zeros_like(parameters[2]))
    totals, (results, token_grads, cond_grads) = lax.scan(one_group, initial, (token_groups, cond_groups, upstream_groups))
    block_out = results.reshape(tokens.shape).astype(jnp.bfloat16)
    tokens_grad = token_grads.reshape(tokens.shape).astype(jnp.bfloat16)
    cond_grad = cond_grads.reshape(condition.shape)
    rows_new, rows_first_new, rows_second_new = adam_step(w_rows, totals[0], rows_first, rows_second, decay_rate)
    down_new, down_first_new, down_second_new = adam_step(w_down, totals[1], down_first, down_second, decay_rate)
    bias_new, bias_first_new, bias_second_new = adam_step(bias_pack, totals[2], bias_first, bias_second, 0.0)
    return (block_out, tokens_grad, cond_grad, rows_new, rows_first_new, rows_second_new, down_new, down_first_new, down_second_new, bias_new, bias_first_new, bias_second_new)
```

```python
from functools import partial

import jax
import jax.numpy as jnp
from jax import lax
from jax.experimental import pallas as pl
from jax.experimental.pallas import tpu as pltpu
from jax.sharding import PartitionSpec as P

HEADS = 6
HEAD = 64
STEP = 10


norm_eps = 1e-06
beta_one = 0.9
beta_two = 0.999
adam_eps = 1e-08
decay_rate = 0.1
learn_rate = 0.1


def normalize(values):
    average = jnp.mean(values, axis=-1, keepdims=True)
    centered = values - average
    variance = jnp.mean(centered * centered, axis=-1, keepdims=True)
    inv_std = lax.rsqrt(variance + norm_eps)
    return (centered * inv_std, inv_std)


def norm_back(gradient, normed, inv_std):
    return inv_std * (
        gradient
        - jnp.mean(gradient, axis=-1, keepdims=True)
        - normed * jnp.mean(gradient * normed, axis=-1, keepdims=True)
    )


def matrix_multiply(spec_text, left, right):
    return jnp.einsum(spec_text, left, right, preferred_element_type=jnp.float32)


def adam_step(weight, gradient, moment_one, moment_two, weight_decay):
    first_new = beta_one * moment_one.astype(jnp.float32) + (1.0 - beta_one) * gradient
    second_new = beta_two * moment_two.astype(jnp.float32) + (1.0 - beta_two) * gradient * gradient
    first_hat = first_new / (1.0 - beta_one**STEP)
    second_hat = second_new / (1.0 - beta_two**STEP)
    master = weight.astype(jnp.float32)
    updated = master - learn_rate * (
        first_hat / (jnp.sqrt(second_hat) + adam_eps) + weight_decay * master
    )
    return (updated, first_new, second_new)


MESH = pl.DeviceIdType.MESH
VMEM_BYTES = 56 * 1024 * 1024
ROW_STEP = 144


class Copies:
    def __init__(self, send_sem, recv_sem):
        self.send_sem, self.recv_sem, self.made = send_sem, recv_sem, []

    def start(self, source, target, device):
        at = len(self.made)
        copy = pltpu.make_async_remote_copy(
            src_ref=source,
            dst_ref=target,
            send_sem=self.send_sem.at[at],
            recv_sem=self.recv_sem.at[at],
            device_id=device,
            device_id_type=MESH,
        )
        copy.start()
        self.made.append(copy)
        return copy

    def finish(self):
        for copy in self.made:
            copy.wait_send()


def meet(peers):
    barrier = pltpu.get_barrier_semaphore()
    for peer in peers:
        pl.semaphore_signal(barrier, inc=1, device_id=peer, device_id_type=MESH)
    pl.semaphore_wait(barrier, len(peers))


def flip(index):
    return index + 1 - 2 * lax.rem(index, 2)


def gather_kernel(
    rows_ref,
    down_ref,
    bias_ref,
    cond_ref,
    silu_ref,
    rows_out,
    down_out,
    bias_out,
    mod_out,
    silu_all,
    part,
    part_in,
    send_sem,
    recv_sem,
    own_sem,
):
    s, r = lax.axis_index("shard"), lax.axis_index("replica")
    x = lax.rem(r, 2)
    core, across, corner = (flip(s), r), (lax.rem(s + 2, 4), r), (flip(lax.rem(s + 2, 4)), r)
    beside = (s, flip(r))
    meet([core, across, corner, beside])
    copies = Copies(send_sem, recv_sem)
    far = across[0]
    columns = rows_ref.shape[1]
    half_rows, half_down = rows_ref.shape[0] // 2, down_ref.shape[0] // 2

    silu_copies = [
        copies.start(silu_ref.at[peer[0]], silu_all.at[s], peer) for peer in (across, corner, core)
    ]

    def pieces(slot, half):
        low = pl.ds(pl.multiple_of(half * half_rows, 16), half_rows)
        low_down = pl.ds(pl.multiple_of(half * half_down, 16), half_down)
        found = []
        for at in range(2):
            cols = pl.ds(at * (columns // 2), columns // 2)
            found.append((rows_ref.at[low, cols], rows_out.at[slot, low, cols]))
        found.append((down_ref.at[low_down], down_out.at[slot, low_down]))
        return found

    bias_far = copies.start(bias_ref, bias_out.at[s], across)
    first = [copies.start(source, target, across) for source, target in pieces(s, x)]
    near = [
        copies.start(bias_ref, bias_out.at[s], core),
        copies.start(rows_ref, rows_out.at[s], core),
        copies.start(down_ref, down_out.at[s], core),
    ]
    own = [
        pltpu.make_async_copy(bias_ref, bias_out.at[s], own_sem.at[0]),
        pltpu.make_async_copy(rows_ref, rows_out.at[s], own_sem.at[1]),
        pltpu.make_async_copy(down_ref, down_out.at[s], own_sem.at[2]),
    ]
    for copy in own:
        copy.start()

    silu_all[s] = silu_ref[s]
    for copy in silu_copies:
        copy.wait_recv()
    depth = cond_ref.shape[0]
    width = part.shape[-1]
    rows = silu_all.shape[0] * silu_all.shape[1]
    left = silu_all[...].reshape(rows, silu_all.shape[2])[:, :depth]
    row = lax.rem(lax.rem(lax.broadcasted_iota(jnp.int32, left.shape, 0), 16), 6)
    total = jnp.zeros((rows, width), jnp.float32)
    for block in range(6):
        chosen = jnp.where(row == block, left, jnp.zeros_like(left))
        total = total + jnp.dot(
            chosen,
            cond_ref[:, block * width : (block + 1) * width],
            preferred_element_type=jnp.float32,
        )
    part[...] = total.reshape(part.shape)
    mod_copies = [
        copies.start(part.at[peer[0]], part_in.at[at], peer)
        for at, peer in enumerate((across, corner, core))
    ]

    bias_far.wait_recv()
    late = [copies.start(bias_out.at[far], bias_out.at[far], core)]
    second = []
    for copy, (_, target) in zip(first, pieces(far, x)):
        copy.wait_recv()
        second.append(copies.start(target, target, beside))
        late.append(copies.start(target, target, core))
    for copy, (_, target) in zip(second, pieces(far, 1 - x)):
        copy.wait_recv()
        late.append(copies.start(target, target, core))
    for copy in mod_copies:
        copy.wait_recv()
    mod_out[...] = part[s] + part_in[0] + part_in[1] + part_in[2]
    for copy in near + late:
        copy.wait_recv()
    for copy in own:
        copy.wait()
    copies.finish()


def gather_weights(w_rows, w_down, bias_pack, silu_cond, shards, replicas):
    latents, width = silu_cond.shape
    own_rows, six_width = w_rows.shape[0], 6 * width
    if shards != 4 or replicas != 8 or latents != 2:
        cond_matrix = lax.all_gather(w_rows[:, :six_width], "shard", axis=0, tiled=True)
        return (
            lax.all_gather(w_rows[:, six_width:], "shard", axis=0, tiled=True),
            lax.all_gather(w_down, "shard", axis=0, tiled=True),
            lax.all_gather(bias_pack, "shard", axis=0, tiled=True),
            matrix_multiply("ld,de->le", silu_cond, cond_matrix),
        )
    spread = silu_cond.reshape(latents, shards, own_rows).transpose(1, 0, 2)
    spread = jnp.repeat(spread, 6, axis=1)
    spread = jnp.pad(spread, ((0, 0), (0, 16 - 6 * latents), (0, 128 - own_rows)))
    bias_tile = jnp.pad(bias_pack, (0, 2048 - bias_pack.shape[0])).reshape(16, 128)
    rows = w_rows[:, six_width:]
    vmem = pl.BlockSpec(memory_space=pltpu.VMEM)
    rows_full, down_full, bias_full, mod = pl.pallas_call(
        gather_kernel,
        out_shape=(
            jax.ShapeDtypeStruct((shards,) + rows.shape, jnp.bfloat16),
            jax.ShapeDtypeStruct((shards,) + w_down.shape, jnp.bfloat16),
            jax.ShapeDtypeStruct((shards, 16, 128), jnp.bfloat16),
            jax.ShapeDtypeStruct((16, width), jnp.float32),
        ),
        in_specs=[vmem] * 5,
        out_specs=(vmem,) * 4,
        scratch_shapes=[
            pltpu.VMEM((shards, 16, 128), jnp.bfloat16),
            pltpu.VMEM((shards, 16, width), jnp.float32),
            pltpu.VMEM((3, 16, width), jnp.float32),
            pltpu.SemaphoreType.DMA((32,)),
            pltpu.SemaphoreType.DMA((32,)),
            pltpu.SemaphoreType.DMA((3,)),
        ],
        compiler_params=pltpu.CompilerParams(
            collective_id=0, has_side_effects=True, vmem_limit_bytes=VMEM_BYTES
        ),
        name="gather_weights",
    )(rows, w_down, bias_tile, w_rows[:, :six_width], spread)
    bias_full = bias_full.reshape(shards, 2048)[:, : bias_pack.shape[0]].reshape(-1)
    return (
        rows_full.reshape(-1, rows.shape[1]),
        down_full.reshape(-1, width),
        bias_full,
        mod[: 6 * latents].reshape(latents, six_width),
    )


def reduce_kernel(
    packed_ref,
    small_ref,
    cond_ref,
    sum_out,
    small_out,
    silu_out,
    core_in,
    core_sum,
    across_in,
    across_sum,
    beside_in,
    beside_sum,
    line_in,
    silu_part,
    send_sem,
    recv_sem,
):
    s, r = lax.axis_index("shard"), lax.axis_index("replica")
    x, z = lax.rem(r, 2), r // 2
    c, y = lax.rem(s, 2), s // 2
    core, across, corner = (flip(s), r), (lax.rem(s + 2, 4), r), (flip(lax.rem(s + 2, 4)), r)
    beside = (s, flip(r))
    line_z = [lax.rem(z + step, 4) for step in (1, 2, 3)]
    line = [(s, 2 * at + x) for at in line_z]
    meet([core, across, corner, beside] + line)
    copies = Copies(send_sem, recv_sem)
    parts = range(3)
    cols = [pl.ds(128 * part, 128) for part in parts]
    whole = packed_ref.shape[1]
    half, share = whole // 2, whole // 8

    def add_rows(count, body):
        def one(step, carry):
            body(pl.multiple_of(step * ROW_STEP, 16))
            return carry

        lax.fori_loop(0, count // ROW_STEP, one, 0)

    def f32(value):
        return value.astype(jnp.float32)

    core_copies = []
    for part in parts:
        core_copies.append(
            [
                copies.start(
                    packed_ref.at[2 * side + 1 - c, :, cols[part]],
                    core_in.at[side, :, cols[part]],
                    core,
                )
                for side in (1 - y, y)
            ]
        )
    small_out[s, x, z] = small_ref[...]
    own_small = small_out.at[s, x, z]
    small_line = [copies.start(own_small, own_small, peer) for peer in line]

    across_copies = []
    for part in parts:
        for at, side in enumerate((1 - y, y)):
            core_copies[part][at].wait_recv()

            def add(low, part=part, side=side):
                rows = pl.ds(low, ROW_STEP)
                core_sum[side, rows, cols[part]] = (
                    f32(packed_ref[2 * side + c, rows, cols[part]])
                    + f32(core_in[side, rows, cols[part]])
                ).astype(jnp.bfloat16)

            add_rows(whole, add)
            if at == 0:
                across_copies.append(
                    copies.start(
                        core_sum.at[side, :, cols[part]], across_in.at[:, cols[part]], across
                    )
                )

    for copy in small_line:
        copy.wait_recv()
    small_beside = copies.start(small_out.at[s, x], small_out.at[s, x], beside)

    beside_copies, line_copies, gather_copies, last_copies = {}, {}, {}, {}

    def stage_beside(part):
        across_copies[part].wait_recv()

        def add(low):
            rows = pl.ds(low, ROW_STEP)
            across_sum[rows, cols[part]] = (
                f32(core_sum[y, rows, cols[part]]) + f32(across_in[rows, cols[part]])
            ).astype(jnp.bfloat16)

        add_rows(whole, add)
        beside_copies[part] = copies.start(
            across_sum.at[pl.ds(pl.multiple_of((1 - x) * half, 16), half), cols[part]],
            beside_in.at[:, cols[part]],
            beside,
        )

    def stage_line(part):
        beside_copies[part].wait_recv()

        def add(low):
            rows = pl.ds(low, ROW_STEP)
            from_rows = pl.ds(pl.multiple_of(x * half + low, 16), ROW_STEP)
            beside_sum[rows, cols[part]] = (
                f32(across_sum[from_rows, cols[part]]) + f32(beside_in[rows, cols[part]])
            ).astype(jnp.bfloat16)

        add_rows(half, add)
        line_copies[part] = [
            copies.start(
                beside_sum.at[pl.ds(pl.multiple_of(line_z[at] * share, 16), share), cols[part]],
                line_in.at[at, :, cols[part]],
                line[at],
            )
            for at in range(3)
        ]

    def stage_gather(part):
        for copy in line_copies[part]:
            copy.wait_recv()
        rows = pl.ds(pl.multiple_of(z * share, 16), share)
        total = f32(beside_sum[rows, cols[part]])
        for at in range(3):
            total = total + f32(line_in[at, :, cols[part]])
        sum_out[x, z, :, cols[part]] = total.astype(jnp.bfloat16)
        own = sum_out.at[x, z, :, cols[part]]
        gather_copies[part] = [copies.start(own, own, peer) for peer in line]
        last_copies[part] = [copies.start(own, own, beside)]

    def stage_last(part):
        for at in range(3):
            gather_copies[part][at].wait_recv()
            origin = lax.rem(z + 3 - at, 4)
            piece = sum_out.at[x, origin, :, cols[part]]
            last_copies[part].append(copies.start(piece, piece, beside))

    stage_beside(0)
    small_beside.wait_recv()
    small_across = copies.start(small_out.at[s], small_out.at[s], across)
    stage_beside(1)
    stage_line(0)
    stage_beside(2)
    stage_line(1)
    stage_gather(0)
    small_across.wait_recv()
    far = across[0]
    small_core = [
        copies.start(small_out.at[s], small_out.at[s], core),
        copies.start(small_out.at[far], small_out.at[far], core),
    ]
    stage_line(2)
    stage_gather(1)
    stage_last(0)

    for copy in small_core:
        copy.wait_recv()
    depth = cond_ref.shape[0]
    width = packed_ref.shape[-1]
    left = jnp.concatenate([small_out[at, x, z, 0:16] for at in range(4)], axis=0)
    row = lax.rem(lax.rem(lax.broadcasted_iota(jnp.int32, left.shape, 0), 16), 6)
    total = jnp.zeros((64, depth), jnp.float32)
    for block in range(6):
        chosen = jnp.where(row == block, left, jnp.zeros_like(left))
        total = total + lax.dot_general(
            chosen,
            cond_ref[:, block * width : (block + 1) * width],
            (((1,), (1,)), ((), ())),
            preferred_element_type=jnp.float32,
        )
    silu_part[...] = jnp.zeros_like(silu_part)
    silu_part[:, :, 0:depth] = total.reshape(4, 16, depth)
    silu_out[s] = silu_part[s]
    silu_copies = [
        copies.start(silu_part.at[peer[0]], silu_out.at[s], peer)
        for peer in (across, corner, core)
    ]
    stage_gather(2)
    stage_last(1)
    stage_last(2)
    for copy in silu_copies:
        copy.wait_recv()
    for part in parts:
        for copy in last_copies[part]:
            copy.wait_recv()
    copies.finish()


def reduce_gradients(
    packed, delta_modulation, silu_cond, bias_local, w_rows, shards, replicas
):
    latents, width = silu_cond.shape
    own_rows, six_width = w_rows.shape[0], 6 * width
    if shards != 4 or replicas != 8 or latents != 2:
        summed = lax.psum_scatter(
            packed.reshape(-1, width).astype(jnp.float32), "shard", scatter_dimension=0, tiled=True
        )
        summed = lax.psum(summed, "replica")
        axes = ("shard", "replica")
        cond_matrix = lax.all_gather(w_rows[:, :six_width], "shard", axis=0, tiled=True)
        return (
            summed,
            lax.all_gather(delta_modulation, axes, axis=0, tiled=True),
            lax.all_gather(silu_cond, axes, axis=0, tiled=True),
            lax.psum(bias_local, axes),
            matrix_multiply("le,de->ld", delta_modulation, cond_matrix),
        )
    whole = packed.shape[1]
    small = jnp.concatenate(
        [
            delta_modulation.reshape(6 * latents, width),
            silu_cond,
            jnp.zeros((16 - 7 * latents, width), jnp.bfloat16),
            bias_local.astype(jnp.bfloat16).reshape(-1, width),
            jnp.zeros((16 - bias_local.shape[0] // width, width), jnp.bfloat16),
        ],
        axis=0,
    )
    vmem = pl.BlockSpec(memory_space=pltpu.VMEM)
    bf16 = jnp.bfloat16
    summed, every, silu_parts = pl.pallas_call(
        reduce_kernel,
        out_shape=(
            jax.ShapeDtypeStruct((2, 4, whole // 8, width), bf16),
            jax.ShapeDtypeStruct((shards, 2, 4, 32, width), bf16),
            jax.ShapeDtypeStruct((shards, 16, 128), jnp.float32),
        ),
        in_specs=[vmem] * 3,
        out_specs=(vmem,) * 3,
        scratch_shapes=[
            pltpu.VMEM((2, whole, width), bf16),
            pltpu.VMEM((2, whole, width), bf16),
            pltpu.VMEM((whole, width), bf16),
            pltpu.VMEM((whole, width), bf16),
            pltpu.VMEM((whole // 2, width), bf16),
            pltpu.VMEM((whole // 2, width), bf16),
            pltpu.VMEM((3, whole // 8, width), bf16),
            pltpu.VMEM((shards, 16, 128), jnp.float32),
            pltpu.SemaphoreType.DMA((64,)),
            pltpu.SemaphoreType.DMA((64,)),
        ],
        compiler_params=pltpu.CompilerParams(
            collective_id=1, has_side_effects=True, vmem_limit_bytes=VMEM_BYTES
        ),
        name="reduce_gradients",
    )(packed, small, w_rows[:, :six_width])
    every = every.transpose(0, 2, 1, 3, 4).reshape(shards * replicas, 32, width)
    bias_rows = every[:, 16 : 16 + bias_local.shape[0] // width]
    delta_silu = silu_parts[:, : 6 * latents, :own_rows]
    delta_silu = delta_silu.reshape(shards, latents, 6, own_rows).sum(axis=2)
    return (
        summed.reshape(whole, width),
        every[:, : 6 * latents].reshape(-1, six_width),
        every[:, 6 * latents : 7 * latents].reshape(-1, width),
        bias_rows.astype(jnp.float32).sum(axis=0).reshape(-1),
        delta_silu.transpose(1, 0, 2).reshape(latents, width),
    )


def per_device(
    shards,
    replicas,
    tokens,
    condition,
    cotangent,
    w_rows,
    w_down,
    bias_pack,
    rows_first,
    rows_second,
    down_first,
    down_second,
    bias_first,
    bias_second,
):
    latents, positions, embedding_width = tokens.shape
    hidden_units_width = w_rows.shape[1] - 10 * embedding_width
    six_width = 6 * embedding_width
    cond_values = condition.astype(jnp.float32)
    silu_cond = jax.nn.silu(cond_values).astype(jnp.bfloat16)
    rows_full, shrink_weight, bias_full, modulation = gather_weights(
        w_rows, w_down, bias_pack, silu_cond, shards, replicas
    )
    bias_entries = bias_full.astype(jnp.float32)
    modulation = modulation + bias_entries[:six_width]
    triple_matrix = rows_full[:, : 3 * embedding_width]
    output_matrix = rows_full[:, 3 * embedding_width : 4 * embedding_width]
    expand_weight = rows_full[:, 4 * embedding_width :]
    blocks_six = [
        modulation[:, None, index * embedding_width : (index + 1) * embedding_width]
        for index in range(6)
    ]
    shift_attention, scale_attention, gate_attention, shift_feed, scale_feed, gate_feed = blocks_six
    token_values = tokens.astype(jnp.float32)
    normed_attention, inv_attention = normalize(token_values)
    input_attention = (normed_attention * (1.0 + scale_attention) + shift_attention).astype(
        jnp.bfloat16
    )
    zeros_key = jnp.zeros((embedding_width,), jnp.float32)
    triple_bias = jnp.concatenate(
        [
            bias_entries[six_width : 7 * embedding_width],
            zeros_key,
            bias_entries[7 * embedding_width : 8 * embedding_width],
        ]
    )
    projected = (
        matrix_multiply("lsd,de->lse", input_attention, triple_matrix) + triple_bias
    ).astype(jnp.bfloat16)
    head_shape = (latents, positions, HEADS, HEAD)
    flat_shape = (latents, positions, embedding_width)
    query = projected[..., :embedding_width].reshape(head_shape)
    keys = projected[..., embedding_width : 2 * embedding_width].reshape(head_shape)
    values = projected[..., 2 * embedding_width :].reshape(head_shape)
    score_scale = HEAD ** (-0.5)
    scores = matrix_multiply("lqhe,lkhe->lhqk", query, keys) * score_scale
    log_total = jax.nn.logsumexp(scores, axis=-1, keepdims=True)
    softmax_low = jnp.exp(scores - log_total).astype(jnp.bfloat16)
    mixed_heads = (
        matrix_multiply("lhqk,lkhe->lqhe", softmax_low, values)
        .reshape(flat_shape)
        .astype(jnp.bfloat16)
    )
    branch = (
        matrix_multiply("lsd,de->lse", mixed_heads, output_matrix)
        + bias_entries[8 * embedding_width : 9 * embedding_width]
    )
    residual = token_values + gate_attention * branch
    normed_feed, inv_feed = normalize(residual)
    feed_input = (normed_feed * (1.0 + scale_feed) + shift_feed).astype(jnp.bfloat16)
    hidden = (
        matrix_multiply("wqg,gc->wqc", feed_input, expand_weight)
        + bias_entries[9 * embedding_width : 9 * embedding_width + hidden_units_width]
    )
    gelu_out, gelu_pull = jax.vjp(partial(jax.nn.gelu, approximate=True), hidden)
    activated_hidden = gelu_out.astype(jnp.bfloat16)
    feed_out = (
        matrix_multiply("wku,ux->wkx", activated_hidden, shrink_weight)
        + bias_entries[9 * embedding_width + hidden_units_width :]
    )
    block_out = (residual + gate_feed * feed_out).astype(jnp.bfloat16)
    upstream = cotangent.astype(jnp.float32)
    delta_gate_feed = jnp.sum(upstream * feed_out, axis=1)
    delta_feed_branch = (gate_feed * upstream).astype(jnp.bfloat16)
    summed_down_weight = matrix_multiply("pxz,pxk->zk", activated_hidden, delta_feed_branch)
    bias_down = jnp.sum(delta_feed_branch.astype(jnp.float32), axis=(0, 1))
    delta_activated = matrix_multiply("tgw,uw->tgu", delta_feed_branch, shrink_weight)
    delta_hidden_units = gelu_pull(delta_activated)[0].astype(jnp.bfloat16)
    summed_expand_weight = matrix_multiply("pce,pcw->ew", feed_input, delta_hidden_units)
    bias_expand = jnp.sum(delta_hidden_units.astype(jnp.float32), axis=(0, 1))
    delta_feed_input = matrix_multiply("kzq,wq->kzw", delta_hidden_units, expand_weight)
    delta_shift_feed = jnp.sum(delta_feed_input, axis=1)
    delta_scale_feed = jnp.sum(delta_feed_input * normed_feed, axis=1)
    delta_residual = upstream + norm_back(
        delta_feed_input * (1.0 + scale_feed), normed_feed, inv_feed
    )
    delta_gate_attention = jnp.sum(delta_residual * branch, axis=1)
    delta_branch = (gate_attention * delta_residual).astype(jnp.bfloat16)
    total_output = matrix_multiply("lsd,lse->de", mixed_heads, delta_branch)
    bias_output = jnp.sum(delta_branch.astype(jnp.float32), axis=(0, 1))
    delta_mixed = (
        matrix_multiply("lse,de->lsd", delta_branch, output_matrix)
        .astype(jnp.bfloat16)
        .reshape(head_shape)
    )
    scores_again = matrix_multiply("lqhe,lkhe->lhqk", query, keys) * score_scale
    softmax_full = jnp.exp(scores_again - log_total)
    softmax_again = softmax_full.astype(jnp.bfloat16)
    delta_soft = matrix_multiply("lqhe,lkhe->lhqk", delta_mixed, values)
    delta_values = matrix_multiply("lhqk,lqhe->lkhe", softmax_again, delta_mixed).astype(
        jnp.bfloat16
    )
    row_inner = jnp.sum(delta_soft * softmax_full, axis=-1, keepdims=True)
    delta_scores = (softmax_full * (delta_soft - row_inner)).astype(jnp.bfloat16)
    delta_query = (matrix_multiply("lhqk,lkhe->lqhe", delta_scores, keys) * score_scale).astype(
        jnp.bfloat16
    )
    delta_keys = (matrix_multiply("lhqk,lqhe->lkhe", delta_scores, query) * score_scale).astype(
        jnp.bfloat16
    )
    delta_projected = jnp.concatenate(
        [
            delta_query.reshape(flat_shape),
            delta_keys.reshape(flat_shape),
            delta_values.reshape(flat_shape),
        ],
        axis=-1,
    )
    total_triple = matrix_multiply("lsd,lse->de", input_attention, delta_projected)
    bias_query = jnp.sum(delta_query.reshape(flat_shape).astype(jnp.float32), axis=(0, 1))
    bias_valued = jnp.sum(delta_values.reshape(flat_shape).astype(jnp.float32), axis=(0, 1))
    delta_input_attention = matrix_multiply("lse,de->lsd", delta_projected, triple_matrix)
    delta_shift_attention = jnp.sum(delta_input_attention, axis=1)
    delta_scale_attention = jnp.sum(delta_input_attention * normed_attention, axis=1)
    delta_tokens = delta_residual + norm_back(
        delta_input_attention * (1.0 + scale_attention), normed_attention, inv_attention
    )
    tokens_grad = delta_tokens.astype(jnp.bfloat16)
    delta_modulation = jnp.concatenate(
        [
            delta_shift_attention,
            delta_scale_attention,
            delta_gate_attention,
            delta_shift_feed,
            delta_scale_feed,
            delta_gate_feed,
        ],
        axis=1,
    ).astype(jnp.bfloat16)
    bias_local = jnp.concatenate([bias_query, bias_valued, bias_output, bias_expand, bias_down])
    total_rows = jnp.concatenate([total_triple, total_output, summed_expand_weight], axis=1)
    blocks = total_rows.shape[1] // embedding_width
    shard_rows = w_rows.shape[0]
    packed_rows = (
        total_rows.astype(jnp.bfloat16)
        .reshape(shards, shard_rows, blocks, embedding_width)
        .transpose(0, 2, 1, 3)
        .reshape(shards, blocks * shard_rows, embedding_width)
    )
    packed_down = summed_down_weight.astype(jnp.bfloat16).reshape(shards, -1, embedding_width)
    packed = jnp.concatenate([packed_rows, packed_down], axis=1)
    summed, every_modulation, every_silu, bias_rest, delta_silu = reduce_gradients(
        packed, delta_modulation, silu_cond, bias_local, w_rows, shards, replicas
    )
    shard_at = lax.axis_index("shard")
    own_silu = lax.dynamic_slice_in_dim(every_silu, shard_at * shard_rows, shard_rows, 1)
    total_cond = matrix_multiply("ld,le->de", own_silu, every_modulation)
    bias_cond = jnp.sum(every_modulation.astype(jnp.float32), axis=0)
    cond_grad = jax.vjp(jax.nn.silu, cond_values)[1](delta_silu)[0]
    split_at = blocks * shard_rows
    own_rows = (
        summed[:split_at]
        .reshape(blocks, shard_rows, embedding_width)
        .transpose(1, 0, 2)
        .reshape(shard_rows, -1)
        .astype(jnp.float32)
    )
    rows_grad = jnp.concatenate([total_cond, own_rows], axis=1)
    down_grad = summed[split_at:].astype(jnp.float32)
    bias_share = bias_pack.shape[0]
    bias_grad = lax.dynamic_slice_in_dim(
        jnp.concatenate([bias_cond, bias_rest]), shard_at * bias_share, bias_share, 0
    )
    rows_new, rows_first_new, rows_second_new = adam_step(
        w_rows, rows_grad, rows_first, rows_second, decay_rate
    )
    down_new, down_first_new, down_second_new = adam_step(
        w_down, down_grad, down_first, down_second, decay_rate
    )
    bias_new, bias_first_new, bias_second_new = adam_step(
        bias_pack, bias_grad, bias_first, bias_second, 0.0
    )
    return (
        block_out,
        tokens_grad,
        cond_grad,
        rows_new,
        rows_first_new,
        rows_second_new,
        down_new,
        down_first_new,
        down_second_new,
        bias_new,
        bias_first_new,
        bias_second_new,
    )


def solution(mesh):
    placed = (
        P(("shard", "replica"), None, None),
        P(("shard", "replica"), None),
        P(("shard", "replica"), None, None),
        P("shard", None),
        P("shard", None),
        P("shard"),
        P("shard", None),
        P("shard", None),
        P("shard", None),
        P("shard", None),
        P("shard"),
        P("shard"),
    )
    return jax.shard_map(
        partial(per_device, mesh.shape["shard"], mesh.shape["replica"]),
        mesh=mesh,
        in_specs=placed,
        out_specs=(
            P(("shard", "replica"), None, None),
            P(("shard", "replica"), None, None),
            P(("shard", "replica"), None),
            P("shard", None),
            P("shard", None),
            P("shard", None),
            P("shard", None),
            P("shard", None),
            P("shard", None),
            P("shard"),
            P("shard"),
            P("shard"),
        ),
        check_vma=False,
    )
```

```python
import math
from functools import partial

import jax
import jax.numpy as jnp
from jax import lax
from jax.experimental import pallas as pl
from jax.experimental.pallas import tpu as pltpu
from jax.sharding import PartitionSpec as P

HEADS = 6
HEAD = 64
STEP = 10


norm_eps = 1e-06
beta_one = 0.9
beta_two = 0.999
adam_eps = 1e-08
decay_rate = 0.1
learn_rate = 0.1


def normalize(values):
    average = jnp.mean(values, axis=-1, keepdims=True)
    centered = values - average
    variance = jnp.mean(centered * centered, axis=-1, keepdims=True)
    inv_std = lax.rsqrt(variance + norm_eps)
    return (centered * inv_std, inv_std)


def norm_back(gradient, normed, inv_std):
    return inv_std * (
        gradient
        - jnp.mean(gradient, axis=-1, keepdims=True)
        - normed * jnp.mean(gradient * normed, axis=-1, keepdims=True)
    )


def matrix_multiply(spec_text, left, right):
    return jnp.einsum(spec_text, left, right, preferred_element_type=jnp.float32)


def adam_step(weight, gradient, moment_one, moment_two, weight_decay):
    first_new = beta_one * moment_one.astype(jnp.float32) + (1.0 - beta_one) * gradient
    second_new = beta_two * moment_two.astype(jnp.float32) + (1.0 - beta_two) * gradient * gradient
    first_hat = first_new / (1.0 - beta_one**STEP)
    second_hat = second_new / (1.0 - beta_two**STEP)
    master = weight.astype(jnp.float32)
    updated = master - learn_rate * (
        first_hat / (jnp.sqrt(second_hat) + adam_eps) + weight_decay * master
    )
    return (updated, first_new, second_new)


MESH = pl.DeviceIdType.MESH
VMEM_BYTES = 56 * 1024 * 1024
ROW_STEP = 144


class Copies:
    def __init__(self, send_sem, recv_sem):
        self.send_sem, self.recv_sem, self.made = send_sem, recv_sem, []

    def start(self, source, target, device):
        at = len(self.made)
        copy = pltpu.make_async_remote_copy(
            src_ref=source,
            dst_ref=target,
            send_sem=self.send_sem.at[at],
            recv_sem=self.recv_sem.at[at],
            device_id=device,
            device_id_type=MESH,
        )
        copy.start()
        self.made.append(copy)
        return copy

    def finish(self):
        for copy in self.made:
            copy.wait_send()


def meet(peers):
    barrier = pltpu.get_barrier_semaphore()
    for peer in peers:
        pl.semaphore_signal(barrier, inc=1, device_id=peer, device_id_type=MESH)
    pl.semaphore_wait(barrier, len(peers))


def flip(index):
    return index + 1 - 2 * lax.rem(index, 2)


def gather_kernel(
    rows_ref,
    down_ref,
    bias_ref,
    cond_ref,
    silu_ref,
    rows_out,
    down_out,
    bias_out,
    mod_out,
    silu_all,
    part,
    part_in,
    send_sem,
    recv_sem,
    own_sem,
):
    s, r = lax.axis_index("shard"), lax.axis_index("replica")
    x = lax.rem(r, 2)
    core, across, corner = (flip(s), r), (lax.rem(s + 2, 4), r), (flip(lax.rem(s + 2, 4)), r)
    beside = (s, flip(r))
    meet([core, across, corner, beside])
    copies = Copies(send_sem, recv_sem)
    far = across[0]
    columns = rows_ref.shape[1]
    half_rows, half_down = rows_ref.shape[0] // 2, down_ref.shape[0] // 2

    silu_copies = [
        copies.start(silu_ref.at[peer[0]], silu_all.at[s], peer) for peer in (across, corner, core)
    ]

    def pieces(slot, half):
        low = pl.ds(pl.multiple_of(half * half_rows, 16), half_rows)
        low_down = pl.ds(pl.multiple_of(half * half_down, 16), half_down)
        found = []
        for at in range(2):
            cols = pl.ds(at * (columns // 2), columns // 2)
            found.append((rows_ref.at[low, cols], rows_out.at[slot, low, cols]))
        found.append((down_ref.at[low_down], down_out.at[slot, low_down]))
        return found

    bias_far = copies.start(bias_ref, bias_out.at[s], across)
    first = [copies.start(source, target, across) for source, target in pieces(s, x)]
    near = [
        copies.start(bias_ref, bias_out.at[s], core),
        copies.start(rows_ref, rows_out.at[s], core),
        copies.start(down_ref, down_out.at[s], core),
    ]
    own = [
        pltpu.make_async_copy(bias_ref, bias_out.at[s], own_sem.at[0]),
        pltpu.make_async_copy(rows_ref, rows_out.at[s], own_sem.at[1]),
        pltpu.make_async_copy(down_ref, down_out.at[s], own_sem.at[2]),
    ]
    for copy in own:
        copy.start()

    silu_all[s] = silu_ref[s]
    for copy in silu_copies:
        copy.wait_recv()
    depth = cond_ref.shape[0]
    width = part.shape[-1]
    rows = silu_all.shape[0] * silu_all.shape[1]
    left = silu_all[...].reshape(rows, silu_all.shape[2])[:, :depth]
    row = lax.rem(lax.rem(lax.broadcasted_iota(jnp.int32, left.shape, 0), 16), 6)
    total = jnp.zeros((rows, width), jnp.float32)
    for block in range(6):
        chosen = jnp.where(row == block, left, jnp.zeros_like(left))
        total = total + jnp.dot(
            chosen,
            cond_ref[:, block * width : (block + 1) * width],
            preferred_element_type=jnp.float32,
        )
    part[...] = total.reshape(part.shape)
    mod_copies = [
        copies.start(part.at[peer[0]], part_in.at[at], peer)
        for at, peer in enumerate((across, corner, core))
    ]

    bias_far.wait_recv()
    late = [copies.start(bias_out.at[far], bias_out.at[far], core)]
    second = []
    for copy, (_, target) in zip(first, pieces(far, x)):
        copy.wait_recv()
        second.append(copies.start(target, target, beside))
        late.append(copies.start(target, target, core))
    for copy, (_, target) in zip(second, pieces(far, 1 - x)):
        copy.wait_recv()
        late.append(copies.start(target, target, core))
    for copy in mod_copies:
        copy.wait_recv()
    mod_out[...] = part[s] + part_in[0] + part_in[1] + part_in[2]
    for copy in near + late:
        copy.wait_recv()
    for copy in own:
        copy.wait()
    copies.finish()


def gather_weights(w_rows, w_down, bias_pack, silu_cond, shards, replicas):
    latents, width = silu_cond.shape
    own_rows, six_width = w_rows.shape[0], 6 * width
    if shards != 4 or replicas != 8 or latents != 2:
        cond_matrix = lax.all_gather(w_rows[:, :six_width], "shard", axis=0, tiled=True)
        return (
            lax.all_gather(w_rows[:, six_width:], "shard", axis=0, tiled=True),
            lax.all_gather(w_down, "shard", axis=0, tiled=True),
            lax.all_gather(bias_pack, "shard", axis=0, tiled=True),
            matrix_multiply("ld,de->le", silu_cond, cond_matrix),
        )
    spread = silu_cond.reshape(latents, shards, own_rows).transpose(1, 0, 2)
    spread = jnp.repeat(spread, 6, axis=1)
    spread = jnp.pad(spread, ((0, 0), (0, 16 - 6 * latents), (0, 128 - own_rows)))
    bias_tile = jnp.pad(bias_pack, (0, 2048 - bias_pack.shape[0])).reshape(16, 128)
    rows = w_rows[:, six_width:]
    vmem = pl.BlockSpec(memory_space=pltpu.VMEM)
    rows_full, down_full, bias_full, mod = pl.pallas_call(
        gather_kernel,
        out_shape=(
            jax.ShapeDtypeStruct((shards,) + rows.shape, jnp.bfloat16),
            jax.ShapeDtypeStruct((shards,) + w_down.shape, jnp.bfloat16),
            jax.ShapeDtypeStruct((shards, 16, 128), jnp.bfloat16),
            jax.ShapeDtypeStruct((16, width), jnp.float32),
        ),
        in_specs=[vmem] * 5,
        out_specs=(vmem,) * 4,
        scratch_shapes=[
            pltpu.VMEM((shards, 16, 128), jnp.bfloat16),
            pltpu.VMEM((shards, 16, width), jnp.float32),
            pltpu.VMEM((3, 16, width), jnp.float32),
            pltpu.SemaphoreType.DMA((32,)),
            pltpu.SemaphoreType.DMA((32,)),
            pltpu.SemaphoreType.DMA((3,)),
        ],
        compiler_params=pltpu.CompilerParams(
            collective_id=0, has_side_effects=True, vmem_limit_bytes=VMEM_BYTES
        ),
        name="gather_weights",
    )(rows, w_down, bias_tile, w_rows[:, :six_width], spread)
    bias_full = bias_full.reshape(shards, 2048)[:, : bias_pack.shape[0]].reshape(-1)
    return (
        rows_full.reshape(-1, rows.shape[1]),
        down_full.reshape(-1, width),
        bias_full,
        mod[: 6 * latents].reshape(latents, six_width),
    )


def dot(left, right, left_dim=1, right_dim=0):
    return lax.dot_general(
        left, right, (((left_dim,), (right_dim,)), ((), ())), preferred_element_type=jnp.float32
    )


def column_sum(values):
    return jnp.sum(values, axis=0, keepdims=True)


def feed_half(
    token_ref, upstream_ref, mod_ref, bias_ref, rows_ref, down_ref,
    out_ref, packed_ref, small,
    input_one, projected, soft, mixed, input_two, active, delta_hidden, delta_feed,
    delta_branch, delta_residual, delta_mixed,
):
    latents, positions, width = token_ref.shape
    heads = width // HEAD

    def one(latent, carry):
        tokens = token_ref[latent].astype(jnp.float32)
        upstream = upstream_ref[latent].astype(jnp.float32)
        shift_one, scale_one, gate_one, shift_two, scale_two, gate_two = (
            mod_ref[latent, at : at + 1] for at in range(6)
        )
        rows = pl.ds(pl.multiple_of(latent * positions, 16), positions)
        normed_one, _ = normalize(tokens)
        first_input = (normed_one * (1.0 + scale_one) + shift_one).astype(jnp.bfloat16)
        input_one[rows] = first_input
        for block in range(3):
            cols = slice(block * width, (block + 1) * width)
            value = dot(first_input, rows_ref[:, cols])
            if block != 1:
                value = value + bias_ref[block // 2 : block // 2 + 1]
            projected[rows, cols] = value.astype(jnp.bfloat16)
        for pair in range(heads // 2):
            two = []
            low = 2 * pair * HEAD
            q2, k2, v2 = (
                projected[rows, at * width + low : at * width + low + 2 * HEAD] for at in range(3)
            )
            for at in range(2):
                here = slice(at * HEAD, (at + 1) * HEAD)
                scores = dot(q2[:, here], k2[:, here], 1, 1) * HEAD ** (-0.5)
                power = jnp.exp(scores - jnp.max(scores, axis=-1, keepdims=True))
                weights = power * (1.0 / jnp.sum(power, axis=-1, keepdims=True))
                soft[latent * heads + 2 * pair + at] = weights
                two.append(dot(weights.astype(jnp.bfloat16), v2[:, here]))
            mixed[rows, low : low + 2 * HEAD] = jnp.concatenate(two, axis=1).astype(jnp.bfloat16)
        branch = dot(mixed[rows, :], rows_ref[:, 3 * width : 4 * width]) + bias_ref[2:3]
        residual = tokens + gate_one * branch
        normed_two, inv_two = normalize(residual)
        second_input = (normed_two * (1.0 + scale_two) + shift_two).astype(jnp.bfloat16)
        input_two[rows] = second_input
        feed_delta = (gate_two * upstream).astype(jnp.bfloat16)
        delta_feed[rows] = feed_delta
        small[23:24] += column_sum(feed_delta.astype(jnp.float32))
        feed_out = jnp.zeros((positions, width), jnp.float32) + bias_ref[7:8]
        delta_input = jnp.zeros((positions, width), jnp.float32)
        root = math.sqrt(2.0 / math.pi)
        for block in range(4):
            cols = slice(block * width, (block + 1) * width)
            expand = rows_ref[:, (4 + block) * width : (5 + block) * width]
            hidden = dot(second_input, expand) + bias_ref[3 + block : 4 + block]
            square = hidden * hidden
            bend = jnp.tanh(root * hidden * (1.0 + 0.044715 * square))
            half = 0.5 + 0.5 * bend
            low_active = (hidden * half).astype(jnp.bfloat16)
            slope = half + hidden * (0.5 * root) * (1.0 - bend * bend) * (
                1.0 + (3.0 * 0.044715) * square
            )
            active[rows, cols] = low_active
            feed_out = feed_out + dot(low_active, down_ref[cols, :])
            low_delta = (dot(feed_delta, down_ref[cols, :], 1, 1) * slope).astype(jnp.bfloat16)
            delta_hidden[rows, cols] = low_delta
            small[19 + block : 20 + block] += column_sum(low_delta.astype(jnp.float32))
            delta_input = delta_input + dot(low_delta, expand, 1, 1)
        out_ref[latent] = (residual + gate_two * feed_out).astype(jnp.bfloat16)
        residual_delta = upstream + norm_back(delta_input * (1.0 + scale_two), normed_two, inv_two)
        delta_residual[rows] = residual_delta
        branch_delta = (gate_one * residual_delta).astype(jnp.bfloat16)
        delta_branch[rows] = branch_delta
        small[18:19] += column_sum(branch_delta.astype(jnp.float32))
        delta_mixed[rows] = dot(branch_delta, rows_ref[:, 3 * width : 4 * width], 1, 1).astype(
            jnp.bfloat16
        )
        small[pl.ds(latent * 6 + 2, 1)] = column_sum(residual_delta * branch)
        small[pl.ds(latent * 6 + 3, 1)] = column_sum(delta_input)
        small[pl.ds(latent * 6 + 4, 1)] = column_sum(delta_input * normed_two)
        small[pl.ds(latent * 6 + 5, 1)] = column_sum(upstream * feed_out)
        return carry

    lax.fori_loop(0, latents, one, 0)
    own_rows = width // 4
    for block in range(4):
        cols = slice(block * width, (block + 1) * width)
        total = dot(active[:, cols], delta_feed[...], 0, 0).astype(jnp.bfloat16)
        packed_ref[block, 8 * own_rows :] = total
        put_block(packed_ref, 4 + block, dot(input_two[...], delta_hidden[:, cols], 0, 0))
    put_block(packed_ref, 3, dot(mixed[...], delta_branch[...], 0, 0))


def put_block(packed_ref, block, total):
    own_rows = total.shape[0] // 4
    for shard in range(4):
        packed_ref[shard, block * own_rows : (block + 1) * own_rows] = total[
            shard * own_rows : (shard + 1) * own_rows
        ].astype(jnp.bfloat16)


def attention_half(
    token_ref, mod_ref, rows_ref, grad_ref, packed_ref, small,
    input_one, projected, soft, delta_residual, delta_mixed, delta_projected,
):
    latents, positions, width = token_ref.shape
    heads = width // HEAD

    def one(latent, carry):
        scale_one = mod_ref[latent, 1:2]
        rows = pl.ds(pl.multiple_of(latent * positions, 16), positions)
        for pair in range(heads // 2):
            low = 2 * pair * HEAD
            q2, k2, v2 = (
                projected[rows, at * width + low : at * width + low + 2 * HEAD] for at in range(3)
            )
            m2 = delta_mixed[rows, low : low + 2 * HEAD]
            found = ([], [], [])
            for at in range(2):
                here = slice(at * HEAD, (at + 1) * HEAD)
                weights = soft[latent * heads + 2 * pair + at]
                delta_soft = dot(m2[:, here], v2[:, here], 1, 1)
                inner = jnp.sum(delta_soft * weights, axis=-1, keepdims=True)
                delta_scores = (weights * (delta_soft - inner)).astype(jnp.bfloat16)
                found[0].append(dot(delta_scores, k2[:, here]) * HEAD ** (-0.5))
                found[1].append(dot(delta_scores, q2[:, here], 0, 0) * HEAD ** (-0.5))
                found[2].append(dot(weights.astype(jnp.bfloat16), m2[:, here], 0, 0))
            for at in range(3):
                delta_projected[rows, at * width + low : at * width + low + 2 * HEAD] = (
                    jnp.concatenate(found[at], axis=1).astype(jnp.bfloat16)
                )
        small[16:17] += column_sum(delta_projected[rows, :width].astype(jnp.float32))
        small[17:18] += column_sum(delta_projected[rows, 2 * width :].astype(jnp.float32))
        delta_input = dot(delta_projected[rows, :], rows_ref[:, : 3 * width], 1, 1)
        normed_one, inv_one = normalize(token_ref[latent].astype(jnp.float32))
        grad_ref[latent] = (
            delta_residual[rows, :]
            + norm_back(delta_input * (1.0 + scale_one), normed_one, inv_one)
        ).astype(jnp.bfloat16)
        small[pl.ds(latent * 6, 1)] = column_sum(delta_input)
        small[pl.ds(latent * 6 + 1, 1)] = column_sum(delta_input * normed_one)
        return carry

    lax.fori_loop(0, latents, one, 0)
    for block in range(3):
        put_block(
            packed_ref,
            block,
            dot(input_one[...], delta_projected[:, block * width : (block + 1) * width], 0, 0),
        )


def block_kernel(
    token_ref, upstream_ref, mod_ref, bias_ref, rows_ref, down_ref, silu_ref,
    out_ref, grad_ref, packed_ref, small_ref,
    small, input_one, projected, soft, mixed, input_two, active, delta_hidden, delta_feed,
    delta_branch, delta_residual, delta_mixed, delta_projected,
):
    small[...] = jnp.zeros_like(small)
    small[12:14] = silu_ref[...].astype(jnp.float32)
    feed_half(
        token_ref, upstream_ref, mod_ref, bias_ref, rows_ref, down_ref,
        out_ref, packed_ref, small,
        input_one, projected, soft, mixed, input_two, active, delta_hidden, delta_feed,
        delta_branch, delta_residual, delta_mixed,
    )
    attention_half(
        token_ref, mod_ref, rows_ref, grad_ref, packed_ref, small,
        input_one, projected, soft, delta_residual, delta_mixed, delta_projected,
    )
    small_ref[...] = small[...].astype(jnp.bfloat16)


def block_gradients(tokens, cotangent, modulation, biases, rows_full, down_full, silu_cond):
    latents, positions, width = tokens.shape
    count, hidden_width = latents * positions, down_full.shape[0]
    own_rows = width // 4
    bf16, f32 = jnp.bfloat16, jnp.float32
    vmem = pl.BlockSpec(memory_space=pltpu.VMEM)
    return pl.pallas_call(
        block_kernel,
        out_shape=(
            jax.ShapeDtypeStruct(tokens.shape, bf16),
            jax.ShapeDtypeStruct(tokens.shape, bf16),
            jax.ShapeDtypeStruct((4, 8 * own_rows + hidden_width // 4, width), bf16),
            jax.ShapeDtypeStruct((32, width), bf16),
        ),
        in_specs=[vmem] * 7,
        out_specs=(vmem,) * 4,
        scratch_shapes=[
            pltpu.VMEM((32, width), f32),
            pltpu.VMEM((count, width), bf16),
            pltpu.VMEM((count, 3 * width), bf16),
            pltpu.VMEM((latents * HEADS, positions, positions), f32),
            pltpu.VMEM((count, width), bf16),
            pltpu.VMEM((count, width), bf16),
            pltpu.VMEM((count, hidden_width), bf16),
            pltpu.VMEM((count, hidden_width), bf16),
            pltpu.VMEM((count, width), bf16),
            pltpu.VMEM((count, width), bf16),
            pltpu.VMEM((count, width), f32),
            pltpu.VMEM((count, width), bf16),
            pltpu.VMEM((count, 3 * width), bf16),
        ],
        compiler_params=pltpu.CompilerParams(vmem_limit_bytes=VMEM_BYTES),
        name="block_gradients",
    )(tokens, cotangent, modulation, biases, rows_full, down_full, silu_cond)


def reduce_kernel(
    packed_ref,
    small_ref,
    cond_ref,
    sum_out,
    small_out,
    silu_out,
    core_in,
    core_sum,
    across_in,
    across_sum,
    beside_in,
    beside_sum,
    line_in,
    silu_part,
    send_sem,
    recv_sem,
):
    s, r = lax.axis_index("shard"), lax.axis_index("replica")
    x, z = lax.rem(r, 2), r // 2
    c, y = lax.rem(s, 2), s // 2
    core, across, corner = (flip(s), r), (lax.rem(s + 2, 4), r), (flip(lax.rem(s + 2, 4)), r)
    beside = (s, flip(r))
    line_z = [lax.rem(z + step, 4) for step in (1, 2, 3)]
    line = [(s, 2 * at + x) for at in line_z]
    meet([core, across, corner, beside] + line)
    copies = Copies(send_sem, recv_sem)
    parts = range(3)
    cols = [pl.ds(128 * part, 128) for part in parts]
    whole = packed_ref.shape[1]
    half, share = whole // 2, whole // 8

    def add_rows(count, body):
        def one(step, carry):
            body(pl.multiple_of(step * ROW_STEP, 16))
            return carry

        lax.fori_loop(0, count // ROW_STEP, one, 0)

    def f32(value):
        return value.astype(jnp.float32)

    core_copies = []
    for part in parts:
        core_copies.append(
            [
                copies.start(
                    packed_ref.at[2 * side + 1 - c, :, cols[part]],
                    core_in.at[side, :, cols[part]],
                    core,
                )
                for side in (1 - y, y)
            ]
        )
    small_out[s, x, z] = small_ref[...]
    own_small = small_out.at[s, x, z]
    small_line = [copies.start(own_small, own_small, peer) for peer in line]

    across_copies = []
    for part in parts:
        for at, side in enumerate((1 - y, y)):
            core_copies[part][at].wait_recv()

            def add(low, part=part, side=side):
                rows = pl.ds(low, ROW_STEP)
                core_sum[side, rows, cols[part]] = (
                    f32(packed_ref[2 * side + c, rows, cols[part]])
                    + f32(core_in[side, rows, cols[part]])
                ).astype(jnp.bfloat16)

            add_rows(whole, add)
            if at == 0:
                across_copies.append(
                    copies.start(
                        core_sum.at[side, :, cols[part]], across_in.at[:, cols[part]], across
                    )
                )

    for copy in small_line:
        copy.wait_recv()
    small_beside = copies.start(small_out.at[s, x], small_out.at[s, x], beside)

    beside_copies, line_copies, gather_copies, last_copies = {}, {}, {}, {}

    def stage_beside(part):
        across_copies[part].wait_recv()

        def add(low):
            rows = pl.ds(low, ROW_STEP)
            across_sum[rows, cols[part]] = (
                f32(core_sum[y, rows, cols[part]]) + f32(across_in[rows, cols[part]])
            ).astype(jnp.bfloat16)

        add_rows(whole, add)
        beside_copies[part] = copies.start(
            across_sum.at[pl.ds(pl.multiple_of((1 - x) * half, 16), half), cols[part]],
            beside_in.at[:, cols[part]],
            beside,
        )

    def stage_line(part):
        beside_copies[part].wait_recv()

        def add(low):
            rows = pl.ds(low, ROW_STEP)
            from_rows = pl.ds(pl.multiple_of(x * half + low, 16), ROW_STEP)
            beside_sum[rows, cols[part]] = (
                f32(across_sum[from_rows, cols[part]]) + f32(beside_in[rows, cols[part]])
            ).astype(jnp.bfloat16)

        add_rows(half, add)
        line_copies[part] = [
            copies.start(
                beside_sum.at[pl.ds(pl.multiple_of(line_z[at] * share, 16), share), cols[part]],
                line_in.at[at, :, cols[part]],
                line[at],
            )
            for at in range(3)
        ]

    def stage_gather(part):
        for copy in line_copies[part]:
            copy.wait_recv()
        rows = pl.ds(pl.multiple_of(z * share, 16), share)
        total = f32(beside_sum[rows, cols[part]])
        for at in range(3):
            total = total + f32(line_in[at, :, cols[part]])
        sum_out[x, z, :, cols[part]] = total.astype(jnp.bfloat16)
        own = sum_out.at[x, z, :, cols[part]]
        gather_copies[part] = [copies.start(own, own, peer) for peer in line]
        last_copies[part] = [copies.start(own, own, beside)]

    def stage_last(part):
        for at in range(3):
            gather_copies[part][at].wait_recv()
            origin = lax.rem(z + 3 - at, 4)
            piece = sum_out.at[x, origin, :, cols[part]]
            last_copies[part].append(copies.start(piece, piece, beside))

    stage_beside(0)
    small_beside.wait_recv()
    small_across = copies.start(small_out.at[s], small_out.at[s], across)
    stage_beside(1)
    stage_line(0)
    stage_beside(2)
    stage_line(1)
    stage_gather(0)
    small_across.wait_recv()
    far = across[0]
    small_core = [
        copies.start(small_out.at[s], small_out.at[s], core),
        copies.start(small_out.at[far], small_out.at[far], core),
    ]
    stage_line(2)
    stage_gather(1)
    stage_last(0)

    for copy in small_core:
        copy.wait_recv()
    depth = cond_ref.shape[0]
    width = packed_ref.shape[-1]
    left = jnp.concatenate([small_out[at, x, z, 0:16] for at in range(4)], axis=0)
    row = lax.rem(lax.rem(lax.broadcasted_iota(jnp.int32, left.shape, 0), 16), 6)
    total = jnp.zeros((64, depth), jnp.float32)
    for block in range(6):
        chosen = jnp.where(row == block, left, jnp.zeros_like(left))
        total = total + lax.dot_general(
            chosen,
            cond_ref[:, block * width : (block + 1) * width],
            (((1,), (1,)), ((), ())),
            preferred_element_type=jnp.float32,
        )
    silu_part[...] = jnp.zeros_like(silu_part)
    silu_part[:, :, 0:depth] = total.reshape(4, 16, depth)
    silu_out[s] = silu_part[s]
    silu_copies = [
        copies.start(silu_part.at[peer[0]], silu_out.at[s], peer)
        for peer in (across, corner, core)
    ]
    stage_gather(2)
    stage_last(1)
    stage_last(2)
    for copy in silu_copies:
        copy.wait_recv()
    for part in parts:
        for copy in last_copies[part]:
            copy.wait_recv()
    copies.finish()


def reduce_gradients(
    packed, small, w_rows, latents, shards, replicas
):
    width = packed.shape[-1]
    own_rows, six_width = w_rows.shape[0], 6 * width
    delta_modulation = small[: 6 * latents].reshape(latents, six_width)
    silu_cond = small[6 * latents : 7 * latents]
    bias_local = small[16:24].astype(jnp.float32).reshape(-1)
    if shards != 4 or replicas != 8 or latents != 2:
        summed = lax.psum_scatter(
            packed.reshape(-1, width).astype(jnp.float32), "shard", scatter_dimension=0, tiled=True
        )
        summed = lax.psum(summed, "replica")
        axes = ("shard", "replica")
        cond_matrix = lax.all_gather(w_rows[:, :six_width], "shard", axis=0, tiled=True)
        return (
            summed,
            lax.all_gather(delta_modulation, axes, axis=0, tiled=True),
            lax.all_gather(silu_cond, axes, axis=0, tiled=True),
            lax.psum(bias_local, axes),
            matrix_multiply("le,de->ld", delta_modulation, cond_matrix),
        )
    whole = packed.shape[1]
    vmem = pl.BlockSpec(memory_space=pltpu.VMEM)
    bf16 = jnp.bfloat16
    summed, every, silu_parts = pl.pallas_call(
        reduce_kernel,
        out_shape=(
            jax.ShapeDtypeStruct((2, 4, whole // 8, width), bf16),
            jax.ShapeDtypeStruct((shards, 2, 4, 32, width), bf16),
            jax.ShapeDtypeStruct((shards, 16, 128), jnp.float32),
        ),
        in_specs=[vmem] * 3,
        out_specs=(vmem,) * 3,
        scratch_shapes=[
            pltpu.VMEM((2, whole, width), bf16),
            pltpu.VMEM((2, whole, width), bf16),
            pltpu.VMEM((whole, width), bf16),
            pltpu.VMEM((whole, width), bf16),
            pltpu.VMEM((whole // 2, width), bf16),
            pltpu.VMEM((whole // 2, width), bf16),
            pltpu.VMEM((3, whole // 8, width), bf16),
            pltpu.VMEM((shards, 16, 128), jnp.float32),
            pltpu.SemaphoreType.DMA((64,)),
            pltpu.SemaphoreType.DMA((64,)),
        ],
        compiler_params=pltpu.CompilerParams(
            collective_id=1, has_side_effects=True, vmem_limit_bytes=VMEM_BYTES
        ),
        name="reduce_gradients",
    )(packed, small, w_rows[:, :six_width])
    every = every.transpose(0, 2, 1, 3, 4).reshape(shards * replicas, 32, width)
    bias_rows = every[:, 16 : 16 + bias_local.shape[0] // width]
    delta_silu = silu_parts[:, : 6 * latents, :own_rows]
    delta_silu = delta_silu.reshape(shards, latents, 6, own_rows).sum(axis=2)
    return (
        summed.reshape(whole, width),
        every[:, : 6 * latents].reshape(-1, six_width),
        every[:, 6 * latents : 7 * latents].reshape(-1, width),
        bias_rows.astype(jnp.float32).sum(axis=0).reshape(-1),
        delta_silu.transpose(1, 0, 2).reshape(latents, width),
    )


def per_device(
    shards,
    replicas,
    tokens,
    condition,
    cotangent,
    w_rows,
    w_down,
    bias_pack,
    rows_first,
    rows_second,
    down_first,
    down_second,
    bias_first,
    bias_second,
):
    latents, positions, embedding_width = tokens.shape
    six_width = 6 * embedding_width
    cond_values = condition.astype(jnp.float32)
    silu_cond = jax.nn.silu(cond_values).astype(jnp.bfloat16)
    rows_full, shrink_weight, bias_full, modulation = gather_weights(
        w_rows, w_down, bias_pack, silu_cond, shards, replicas
    )
    bias_entries = bias_full.astype(jnp.float32)
    modulation = modulation + bias_entries[:six_width]
    modulation = jnp.pad(
        modulation.reshape(latents, 6, embedding_width), ((0, 0), (0, 2), (0, 0))
    )
    block_out, tokens_grad, packed, small = block_gradients(
        tokens,
        cotangent,
        modulation,
        bias_entries[six_width:].reshape(-1, embedding_width),
        rows_full,
        shrink_weight,
        silu_cond,
    )
    summed, every_modulation, every_silu, bias_rest, delta_silu = reduce_gradients(
        packed, small, w_rows, latents, shards, replicas
    )
    blocks = rows_full.shape[1] // embedding_width
    shard_rows = w_rows.shape[0]
    shard_at = lax.axis_index("shard")
    own_silu = lax.dynamic_slice_in_dim(every_silu, shard_at * shard_rows, shard_rows, 1)
    total_cond = matrix_multiply("ld,le->de", own_silu, every_modulation)
    bias_cond = jnp.sum(every_modulation.astype(jnp.float32), axis=0)
    cond_grad = jax.vjp(jax.nn.silu, cond_values)[1](delta_silu)[0]
    split_at = blocks * shard_rows
    own_rows = (
        summed[:split_at]
        .reshape(blocks, shard_rows, embedding_width)
        .transpose(1, 0, 2)
        .reshape(shard_rows, -1)
        .astype(jnp.float32)
    )
    rows_grad = jnp.concatenate([total_cond, own_rows], axis=1)
    down_grad = summed[split_at:].astype(jnp.float32)
    bias_share = bias_pack.shape[0]
    bias_grad = lax.dynamic_slice_in_dim(
        jnp.concatenate([bias_cond, bias_rest]), shard_at * bias_share, bias_share, 0
    )
    rows_new, rows_first_new, rows_second_new = adam_step(
        w_rows, rows_grad, rows_first, rows_second, decay_rate
    )
    down_new, down_first_new, down_second_new = adam_step(
        w_down, down_grad, down_first, down_second, decay_rate
    )
    bias_new, bias_first_new, bias_second_new = adam_step(
        bias_pack, bias_grad, bias_first, bias_second, 0.0
    )
    return (
        block_out,
        tokens_grad,
        cond_grad,
        rows_new,
        rows_first_new,
        rows_second_new,
        down_new,
        down_first_new,
        down_second_new,
        bias_new,
        bias_first_new,
        bias_second_new,
    )


def solution(mesh):
    placed = (
        P(("shard", "replica"), None, None),
        P(("shard", "replica"), None),
        P(("shard", "replica"), None, None),
        P("shard", None),
        P("shard", None),
        P("shard"),
        P("shard", None),
        P("shard", None),
        P("shard", None),
        P("shard", None),
        P("shard"),
        P("shard"),
    )
    return jax.shard_map(
        partial(per_device, mesh.shape["shard"], mesh.shape["replica"]),
        mesh=mesh,
        in_specs=placed,
        out_specs=(
            P(("shard", "replica"), None, None),
            P(("shard", "replica"), None, None),
            P(("shard", "replica"), None),
            P("shard", None),
            P("shard", None),
            P("shard", None),
            P("shard", None),
            P("shard", None),
            P("shard", None),
            P("shard"),
            P("shard"),
            P("shard"),
        ),
        check_vma=False,
    )
```

```python
import math
from functools import partial

import jax
import jax.numpy as jnp
from jax import lax
from jax.experimental import pallas as pl
from jax.experimental.pallas import tpu as pltpu
from jax.sharding import PartitionSpec as P

HEADS = 6
HEAD = 64
STEP = 10


norm_eps = 1e-06
beta_one = 0.9
beta_two = 0.999
adam_eps = 1e-08
decay_rate = 0.1
learn_rate = 0.1


def normalize(values):
    average = jnp.mean(values, axis=-1, keepdims=True)
    centered = values - average
    variance = jnp.mean(centered * centered, axis=-1, keepdims=True)
    inv_std = lax.rsqrt(variance + norm_eps)
    return (centered * inv_std, inv_std)


def norm_back(gradient, normed, inv_std):
    return inv_std * (
        gradient
        - jnp.mean(gradient, axis=-1, keepdims=True)
        - normed * jnp.mean(gradient * normed, axis=-1, keepdims=True)
    )


def matrix_multiply(spec_text, left, right):
    return jnp.einsum(spec_text, left, right, preferred_element_type=jnp.float32)


def adam_step(weight, gradient, moment_one, moment_two, weight_decay):
    first_new = beta_one * moment_one.astype(jnp.float32) + (1.0 - beta_one) * gradient
    second_new = beta_two * moment_two.astype(jnp.float32) + (1.0 - beta_two) * gradient * gradient
    first_hat = first_new / (1.0 - beta_one**STEP)
    second_hat = second_new / (1.0 - beta_two**STEP)
    master = weight.astype(jnp.float32)
    updated = master - learn_rate * (
        first_hat / (jnp.sqrt(second_hat) + adam_eps) + weight_decay * master
    )
    return (updated, first_new, second_new)


MESH = pl.DeviceIdType.MESH
VMEM_BYTES = 56 * 1024 * 1024
ROW_STEP = 144


class Copies:
    def __init__(self, send_sem, recv_sem):
        self.send_sem, self.recv_sem, self.made = send_sem, recv_sem, []

    def start(self, source, target, device):
        at = len(self.made)
        copy = pltpu.make_async_remote_copy(
            src_ref=source,
            dst_ref=target,
            send_sem=self.send_sem.at[at],
            recv_sem=self.recv_sem.at[at],
            device_id=device,
            device_id_type=MESH,
        )
        copy.start()
        self.made.append(copy)
        return copy

    def finish(self):
        for copy in self.made:
            copy.wait_send()


def meet(peers):
    barrier = pltpu.get_barrier_semaphore()
    for peer in peers:
        pl.semaphore_signal(barrier, inc=1, device_id=peer, device_id_type=MESH)
    pl.semaphore_wait(barrier, len(peers))


def flip(index):
    return index + 1 - 2 * lax.rem(index, 2)


def gather_kernel(
    rows_ref,
    down_ref,
    bias_ref,
    silu_ref,
    rows_out,
    down_out,
    bias_out,
    mod_out,
    silu_all,
    part,
    part_in,
    send_sem,
    recv_sem,
    own_sem,
):
    s, r = lax.axis_index("shard"), lax.axis_index("replica")
    x = lax.rem(r, 2)
    core, across, corner = (flip(s), r), (lax.rem(s + 2, 4), r), (flip(lax.rem(s + 2, 4)), r)
    beside = (s, flip(r))
    meet([core, across, corner, beside])
    copies = Copies(send_sem, recv_sem)
    far = across[0]
    skip = 6 * mod_out.shape[1]
    columns = rows_ref.shape[1] - skip
    kept = rows_ref.at[:, pl.ds(skip, columns)]
    cond_ref = rows_ref
    half_rows, half_down = rows_ref.shape[0] // 2, down_ref.shape[0] // 2

    silu_copies = [
        copies.start(silu_ref.at[peer[0]], silu_all.at[s], peer) for peer in (across, corner, core)
    ]

    def pieces(slot, half):
        low = pl.ds(pl.multiple_of(half * half_rows, 16), half_rows)
        low_down = pl.ds(pl.multiple_of(half * half_down, 16), half_down)
        found = []
        for at in range(2):
            cols = pl.ds(at * (columns // 2), columns // 2)
            from_cols = pl.ds(skip + at * (columns // 2), columns // 2)
            found.append((rows_ref.at[low, from_cols], rows_out.at[slot, low, cols]))
        found.append((down_ref.at[low_down], down_out.at[slot, low_down]))
        return found

    bias_far = copies.start(bias_ref, bias_out.at[s], across)
    first = [copies.start(source, target, across) for source, target in pieces(s, x)]
    near = [
        copies.start(bias_ref, bias_out.at[s], core),
        copies.start(kept, rows_out.at[s], core),
        copies.start(down_ref, down_out.at[s], core),
    ]
    own = [
        pltpu.make_async_copy(bias_ref, bias_out.at[s], own_sem.at[0]),
        pltpu.make_async_copy(kept, rows_out.at[s], own_sem.at[1]),
        pltpu.make_async_copy(down_ref, down_out.at[s], own_sem.at[2]),
    ]
    for copy in own:
        copy.start()

    silu_all[s] = silu_ref[s]
    for copy in silu_copies:
        copy.wait_recv()
    depth = cond_ref.shape[0]
    width = part.shape[-1]
    rows = silu_all.shape[0] * silu_all.shape[1]
    left = silu_all[...].reshape(rows, silu_all.shape[2])[:, :depth]
    row = lax.rem(lax.rem(lax.broadcasted_iota(jnp.int32, left.shape, 0), 16), 6)
    total = jnp.zeros((rows, width), jnp.float32)
    for block in range(6):
        chosen = jnp.where(row == block, left, jnp.zeros_like(left))
        total = total + jnp.dot(
            chosen,
            cond_ref[:, block * width : (block + 1) * width],
            preferred_element_type=jnp.float32,
        )
    part[...] = total.reshape(part.shape)
    mod_copies = [
        copies.start(part.at[peer[0]], part_in.at[at], peer)
        for at, peer in enumerate((across, corner, core))
    ]

    bias_far.wait_recv()
    late = [copies.start(bias_out.at[far], bias_out.at[far], core)]
    second = []
    for copy, (_, target) in zip(first, pieces(far, x)):
        copy.wait_recv()
        second.append(copies.start(target, target, beside))
        late.append(copies.start(target, target, core))
    for copy, (_, target) in zip(second, pieces(far, 1 - x)):
        copy.wait_recv()
        late.append(copies.start(target, target, core))
    for copy in mod_copies:
        copy.wait_recv()
    mod_out[...] = part[s] + part_in[0] + part_in[1] + part_in[2]
    for copy in near + late:
        copy.wait_recv()
    for copy in own:
        copy.wait()
    copies.finish()


def gather_weights(w_rows, w_down, bias_pack, silu_cond, shards, replicas):
    latents, width = silu_cond.shape
    own_rows, six_width = w_rows.shape[0], 6 * width
    if shards != 4 or replicas != 8 or latents != 2:
        cond_matrix = lax.all_gather(w_rows[:, :six_width], "shard", axis=0, tiled=True)
        return (
            lax.all_gather(w_rows[:, six_width:], "shard", axis=0, tiled=True),
            lax.all_gather(w_down, "shard", axis=0, tiled=True),
            lax.all_gather(bias_pack, "shard", axis=0, tiled=True),
            matrix_multiply("ld,de->le", silu_cond, cond_matrix),
        )
    spread = silu_cond.reshape(latents, shards, own_rows).transpose(1, 0, 2)
    spread = jnp.repeat(spread, 6, axis=1)
    spread = jnp.pad(spread, ((0, 0), (0, 16 - 6 * latents), (0, 128 - own_rows)))
    bias_tile = jnp.pad(bias_pack, (0, 2048 - bias_pack.shape[0])).reshape(16, 128)
    columns = w_rows.shape[1] - six_width
    vmem = pl.BlockSpec(memory_space=pltpu.VMEM)
    rows_full, down_full, bias_full, mod = pl.pallas_call(
        gather_kernel,
        out_shape=(
            jax.ShapeDtypeStruct((shards, own_rows, columns), jnp.bfloat16),
            jax.ShapeDtypeStruct((shards,) + w_down.shape, jnp.bfloat16),
            jax.ShapeDtypeStruct((shards, 16, 128), jnp.bfloat16),
            jax.ShapeDtypeStruct((16, width), jnp.float32),
        ),
        in_specs=[vmem] * 4,
        out_specs=(vmem,) * 4,
        scratch_shapes=[
            pltpu.VMEM((shards, 16, 128), jnp.bfloat16),
            pltpu.VMEM((shards, 16, width), jnp.float32),
            pltpu.VMEM((3, 16, width), jnp.float32),
            pltpu.SemaphoreType.DMA((32,)),
            pltpu.SemaphoreType.DMA((32,)),
            pltpu.SemaphoreType.DMA((3,)),
        ],
        compiler_params=pltpu.CompilerParams(
            collective_id=0, has_side_effects=True, vmem_limit_bytes=VMEM_BYTES
        ),
        name="gather_weights",
    )(w_rows, w_down, bias_tile, spread)
    bias_full = bias_full.reshape(shards, 2048)[:, : bias_pack.shape[0]].reshape(-1)
    return (
        rows_full.reshape(-1, columns),
        down_full.reshape(-1, width),
        bias_full,
        mod[: 6 * latents].reshape(latents, six_width),
    )


def dot(left, right, left_dim=1, right_dim=0):
    return lax.dot_general(
        left, right, (((left_dim,), (right_dim,)), ((), ())), preferred_element_type=jnp.float32
    )


def column_sum(values):
    return jnp.sum(values, axis=0, keepdims=True)


def feed_half(
    token_ref, upstream_ref, mod_ref, bias_ref, rows_ref, down_ref,
    out_ref, packed_ref, small,
    input_one, projected, soft, mixed, input_two, active, delta_hidden, delta_feed,
    delta_branch, delta_residual, delta_mixed,
):
    latents, positions, width = token_ref.shape
    heads = width // HEAD

    def one(latent, carry):
        tokens = token_ref[latent].astype(jnp.float32)
        upstream = upstream_ref[latent].astype(jnp.float32)
        shift_one, scale_one, gate_one, shift_two, scale_two, gate_two = (
            mod_ref[latent, at : at + 1] for at in range(6)
        )
        rows = pl.ds(pl.multiple_of(latent * positions, 16), positions)
        normed_one, _ = normalize(tokens)
        first_input = (normed_one * (1.0 + scale_one) + shift_one).astype(jnp.bfloat16)
        input_one[rows] = first_input
        for block in range(3):
            cols = slice(block * width, (block + 1) * width)
            value = dot(first_input, rows_ref[:, cols])
            if block != 1:
                value = value + bias_ref[block // 2 : block // 2 + 1]
            projected[rows, cols] = value.astype(jnp.bfloat16)
        for pair in range(heads // 2):
            two = []
            low = 2 * pair * HEAD
            q2, k2, v2 = (
                projected[rows, at * width + low : at * width + low + 2 * HEAD] for at in range(3)
            )
            for at in range(2):
                here = slice(at * HEAD, (at + 1) * HEAD)
                scores = dot(q2[:, here], k2[:, here], 1, 1) * HEAD ** (-0.5)
                power = jnp.exp(scores - jnp.max(scores, axis=-1, keepdims=True))
                weights = power * (1.0 / jnp.sum(power, axis=-1, keepdims=True))
                soft[latent * heads + 2 * pair + at] = weights
                two.append(dot(weights.astype(jnp.bfloat16), v2[:, here]))
            mixed[rows, low : low + 2 * HEAD] = jnp.concatenate(two, axis=1).astype(jnp.bfloat16)
        branch = dot(mixed[rows, :], rows_ref[:, 3 * width : 4 * width]) + bias_ref[2:3]
        residual = tokens + gate_one * branch
        normed_two, inv_two = normalize(residual)
        second_input = (normed_two * (1.0 + scale_two) + shift_two).astype(jnp.bfloat16)
        input_two[rows] = second_input
        feed_delta = (gate_two * upstream).astype(jnp.bfloat16)
        delta_feed[rows] = feed_delta
        small[23:24] += column_sum(feed_delta.astype(jnp.float32))
        feed_out = jnp.zeros((positions, width), jnp.float32) + bias_ref[7:8]
        delta_input = jnp.zeros((positions, width), jnp.float32)
        root = math.sqrt(2.0 / math.pi)
        for block in range(4):
            cols = slice(block * width, (block + 1) * width)
            expand = rows_ref[:, (4 + block) * width : (5 + block) * width]
            hidden = dot(second_input, expand) + bias_ref[3 + block : 4 + block]
            square = hidden * hidden
            bend = jnp.tanh(root * hidden * (1.0 + 0.044715 * square))
            half = 0.5 + 0.5 * bend
            low_active = (hidden * half).astype(jnp.bfloat16)
            slope = half + hidden * (0.5 * root) * (1.0 - bend * bend) * (
                1.0 + (3.0 * 0.044715) * square
            )
            active[rows, cols] = low_active
            feed_out = feed_out + dot(low_active, down_ref[cols, :])
            low_delta = (dot(feed_delta, down_ref[cols, :], 1, 1) * slope).astype(jnp.bfloat16)
            delta_hidden[rows, cols] = low_delta
            small[19 + block : 20 + block] += column_sum(low_delta.astype(jnp.float32))
            delta_input = delta_input + dot(low_delta, expand, 1, 1)
        out_ref[latent] = (residual + gate_two * feed_out).astype(jnp.bfloat16)
        residual_delta = upstream + norm_back(delta_input * (1.0 + scale_two), normed_two, inv_two)
        delta_residual[rows] = residual_delta
        branch_delta = (gate_one * residual_delta).astype(jnp.bfloat16)
        delta_branch[rows] = branch_delta
        small[18:19] += column_sum(branch_delta.astype(jnp.float32))
        delta_mixed[rows] = dot(branch_delta, rows_ref[:, 3 * width : 4 * width], 1, 1).astype(
            jnp.bfloat16
        )
        small[pl.ds(latent * 6 + 2, 1)] = column_sum(residual_delta * branch)
        small[pl.ds(latent * 6 + 3, 1)] = column_sum(delta_input)
        small[pl.ds(latent * 6 + 4, 1)] = column_sum(delta_input * normed_two)
        small[pl.ds(latent * 6 + 5, 1)] = column_sum(upstream * feed_out)
        return carry

    lax.fori_loop(0, latents, one, 0)
    own_rows = width // 4
    for block in range(4):
        cols = slice(block * width, (block + 1) * width)
        total = dot(active[:, cols], delta_feed[...], 0, 0).astype(jnp.bfloat16)
        packed_ref[block, 8 * own_rows :] = total
        put_block(packed_ref, 4 + block, dot(input_two[...], delta_hidden[:, cols], 0, 0))


def put_block(packed_ref, block, total):
    own_rows = total.shape[0] // 4
    for shard in range(4):
        packed_ref[shard, block * own_rows : (block + 1) * own_rows] = total[
            shard * own_rows : (shard + 1) * own_rows
        ].astype(jnp.bfloat16)


def attention_latent(
    latent, token_ref, mod_ref, rows_ref, grad_ref, small,
    projected, soft, delta_residual, delta_mixed, delta_projected,
):
    positions, width = token_ref.shape[1:]
    heads = width // HEAD
    scale_one = mod_ref[latent, 1:2]
    rows = pl.ds(pl.multiple_of(latent * positions, 16), positions)
    for pair in range(heads // 2):
        low = 2 * pair * HEAD
        q2, k2, v2 = (
            projected[rows, at * width + low : at * width + low + 2 * HEAD] for at in range(3)
        )
        m2 = delta_mixed[rows, low : low + 2 * HEAD]
        found = ([], [], [])
        for at in range(2):
            here = slice(at * HEAD, (at + 1) * HEAD)
            weights = soft[latent * heads + 2 * pair + at]
            delta_soft = dot(m2[:, here], v2[:, here], 1, 1)
            inner = jnp.sum(delta_soft * weights, axis=-1, keepdims=True)
            delta_scores = (weights * (delta_soft - inner)).astype(jnp.bfloat16)
            found[0].append(dot(delta_scores, k2[:, here]) * HEAD ** (-0.5))
            found[1].append(dot(delta_scores, q2[:, here], 0, 0) * HEAD ** (-0.5))
            found[2].append(dot(weights.astype(jnp.bfloat16), m2[:, here], 0, 0))
        for at in range(3):
            delta_projected[rows, at * width + low : at * width + low + 2 * HEAD] = (
                jnp.concatenate(found[at], axis=1).astype(jnp.bfloat16)
            )
    small[16:17] += column_sum(delta_projected[rows, :width].astype(jnp.float32))
    small[17:18] += column_sum(delta_projected[rows, 2 * width :].astype(jnp.float32))
    delta_input = dot(delta_projected[rows, :], rows_ref[:, : 3 * width], 1, 1)
    normed_one, inv_one = normalize(token_ref[latent].astype(jnp.float32))
    grad_ref[latent] = (
        delta_residual[rows, :]
        + norm_back(delta_input * (1.0 + scale_one), normed_one, inv_one)
    ).astype(jnp.bfloat16)
    small[pl.ds(latent * 6, 1)] = column_sum(delta_input)
    small[pl.ds(latent * 6 + 1, 1)] = column_sum(delta_input * normed_one)


def attention_grads(packed_ref, input_one, delta_projected):
    width = input_one.shape[1]
    for block in range(3):
        put_block(
            packed_ref,
            block,
            dot(input_one[...], delta_projected[:, block * width : (block + 1) * width], 0, 0),
        )


def fused_kernel(
    token_ref, upstream_ref, mod_ref, bias_ref, rows_ref, down_ref, silu_ref, cond_ref,
    out_ref, grad_ref, sum_out, small_out, silu_out,
    small, input_one, projected, soft, mixed, input_two, active, delta_hidden, delta_feed,
    delta_branch, delta_residual, delta_mixed, delta_projected,
    packed_ref, small_low, core_in, core_sum, across_in, across_sum, beside_in, beside_sum,
    line_in, silu_part, send_sem, recv_sem,
):
    s, r = lax.axis_index("shard"), lax.axis_index("replica")
    x, z = lax.rem(r, 2), r // 2
    c, y = lax.rem(s, 2), s // 2
    core, across, corner = (flip(s), r), (lax.rem(s + 2, 4), r), (flip(lax.rem(s + 2, 4)), r)
    beside = (s, flip(r))
    line_z = [lax.rem(z + step, 4) for step in (1, 2, 3)]
    line = [(s, 2 * at + x) for at in line_z]
    meet([core, across, corner, beside] + line)
    copies = Copies(send_sem, recv_sem)
    split, whole, width = 4 * 96, packed_ref.shape[1], packed_ref.shape[2]
    parts = [(split, whole - split, 128 * at, 128) for at in range(3)] + [(0, split, 0, width)]

    def span(first, count):
        return pl.ds(pl.multiple_of(first, 16), count)

    def add_rows(count, body):
        def one(step, carry):
            body(step * 96)
            return carry

        lax.fori_loop(0, count // 96, one, 0)

    def f32(value):
        return value.astype(jnp.float32)

    made = {}

    def start_core(part):
        first, count, left, columns = parts[part]
        rows, cols = pl.ds(first, count), pl.ds(left, columns)
        made["core", part] = [
            copies.start(
                packed_ref.at[2 * side + 1 - c, rows, cols], core_in.at[side, rows, cols], core
            )
            for side in (1 - y, y)
        ]

    def stage_across(part):
        first, count, left, columns = parts[part]
        cols = pl.ds(left, columns)
        for at, side in enumerate((1 - y, y)):
            made["core", part][at].wait_recv()

            def add(low, side=side):
                rows = span(first + low, 96)
                core_sum[side, rows, cols] = (
                    f32(packed_ref[2 * side + c, rows, cols]) + f32(core_in[side, rows, cols])
                ).astype(jnp.bfloat16)

            add_rows(count, add)
            if at == 0:
                rows = pl.ds(first, count)
                made["across", part] = copies.start(
                    core_sum.at[side, rows, cols], across_in.at[rows, cols], across
                )

    def stage_beside(part):
        first, count, left, columns = parts[part]
        cols, half = pl.ds(left, columns), count // 2
        made["across", part].wait_recv()

        def add(low):
            rows = span(first + low, 96)
            across_sum[rows, cols] = (
                f32(core_sum[y, rows, cols]) + f32(across_in[rows, cols])
            ).astype(jnp.bfloat16)

        add_rows(count, add)
        made["beside", part] = copies.start(
            across_sum.at[span(first + (1 - x) * half, half), cols],
            beside_in.at[pl.ds(first, half), cols],
            beside,
        )

    def stage_line(part):
        first, count, left, columns = parts[part]
        cols, half, share = pl.ds(left, columns), count // 2, count // 8
        made["beside", part].wait_recv()

        def add(low):
            rows = span(first + low, 96)
            beside_sum[rows, cols] = (
                f32(across_sum[span(first + x * half + low, 96), cols])
                + f32(beside_in[rows, cols])
            ).astype(jnp.bfloat16)

        add_rows(half, add)
        made["line", part] = [
            copies.start(
                beside_sum.at[span(first + line_z[at] * share, share), cols],
                line_in.at[at, pl.ds(first, share), cols],
                line[at],
            )
            for at in range(3)
        ]

    def stage_gather(part):
        first, count, left, columns = parts[part]
        cols, half, share = pl.ds(left, columns), count // 2, count // 8
        for copy in made["line", part]:
            copy.wait_recv()
        total = f32(beside_sum[span(first + z * share, share), cols])
        for at in range(3):
            total = total + f32(line_in[at, pl.ds(first, share), cols])
        rows = span(first + x * half + z * share, share)
        sum_out[rows, cols] = total.astype(jnp.bfloat16)
        own = sum_out.at[rows, cols]
        made["gather", part] = [copies.start(own, own, peer) for peer in line]
        made["last", part] = [copies.start(own, own, beside)]

    def stage_last(part):
        first, count, left, columns = parts[part]
        cols, half, share = pl.ds(left, columns), count // 2, count // 8
        for at in range(3):
            made["gather", part][at].wait_recv()
            origin = lax.rem(z + 3 - at, 4)
            piece = sum_out.at[span(first + x * half + origin * share, share), cols]
            made["last", part].append(copies.start(piece, piece, beside))

    def attention(latent):
        attention_latent(
            latent, token_ref, mod_ref, rows_ref, grad_ref, small,
            projected, soft, delta_residual, delta_mixed, delta_projected,
        )

    small[...] = jnp.zeros_like(small)
    small[12:14] = silu_ref[...].astype(jnp.float32)
    feed_half(
        token_ref, upstream_ref, mod_ref, bias_ref, rows_ref, down_ref,
        out_ref, packed_ref, small,
        input_one, projected, soft, mixed, input_two, active, delta_hidden, delta_feed,
        delta_branch, delta_residual, delta_mixed,
    )
    for part in range(3):
        start_core(part)
    put_block(packed_ref, 3, dot(mixed[...], delta_branch[...], 0, 0))
    for part in range(3):
        stage_across(part)
    attention(0)
    stage_beside(0)
    attention(1)
    stage_beside(1)
    stage_line(0)
    small_low[...] = small[...].astype(jnp.bfloat16)
    small_out[s, x, z] = small_low[...]
    small_line = [copies.start(small_low, small_out.at[s, x, z], peer) for peer in line]
    attention_grads(packed_ref, input_one, delta_projected)
    start_core(3)
    stage_beside(2)
    stage_line(1)
    stage_across(3)
    for copy in small_line:
        copy.wait_recv()
    small_beside = copies.start(small_out.at[s, x], small_out.at[s, x], beside)
    stage_gather(0)
    stage_line(2)
    small_beside.wait_recv()
    small_across = copies.start(small_out.at[s], small_out.at[s], across)
    stage_gather(1)
    stage_last(0)
    stage_beside(3)
    stage_gather(2)
    stage_last(1)
    stage_line(3)
    small_across.wait_recv()
    far = across[0]
    small_core = [
        copies.start(small_out.at[s], small_out.at[s], core),
        copies.start(small_out.at[far], small_out.at[far], core),
    ]
    stage_last(2)
    for copy in small_core:
        copy.wait_recv()
    depth = cond_ref.shape[0]
    left = jnp.concatenate([small_out[at, x, z, 0:16] for at in range(4)], axis=0)
    row = lax.rem(lax.rem(lax.broadcasted_iota(jnp.int32, left.shape, 0), 16), 6)
    total = jnp.zeros((64, depth), jnp.float32)
    for block in range(6):
        chosen = jnp.where(row == block, left, jnp.zeros_like(left))
        total = total + dot(chosen, cond_ref[:, block * width : (block + 1) * width], 1, 1)
    silu_part[...] = jnp.zeros_like(silu_part)
    silu_part[:, :, 0:depth] = total.reshape(4, 16, depth)
    silu_out[s] = silu_part[s]
    silu_copies = [
        copies.start(silu_part.at[peer[0]], silu_out.at[s], peer)
        for peer in (across, corner, core)
    ]
    stage_gather(3)
    stage_last(3)
    for copy in silu_copies:
        copy.wait_recv()
    for part in range(4):
        for copy in made["last", part]:
            copy.wait_recv()
    copies.finish()


def block_kernel(
    token_ref, upstream_ref, mod_ref, bias_ref, rows_ref, down_ref, silu_ref,
    out_ref, grad_ref, packed_ref, small_ref,
    small, input_one, projected, soft, mixed, input_two, active, delta_hidden, delta_feed,
    delta_branch, delta_residual, delta_mixed, delta_projected,
):
    small[...] = jnp.zeros_like(small)
    small[12:14] = silu_ref[...].astype(jnp.float32)
    feed_half(
        token_ref, upstream_ref, mod_ref, bias_ref, rows_ref, down_ref,
        out_ref, packed_ref, small,
        input_one, projected, soft, mixed, input_two, active, delta_hidden, delta_feed,
        delta_branch, delta_residual, delta_mixed,
    )
    put_block(packed_ref, 3, dot(mixed[...], delta_branch[...], 0, 0))
    for latent in range(token_ref.shape[0]):
        attention_latent(
            latent, token_ref, mod_ref, rows_ref, grad_ref, small,
            projected, soft, delta_residual, delta_mixed, delta_projected,
        )
    attention_grads(packed_ref, input_one, delta_projected)
    small_ref[...] = small[...].astype(jnp.bfloat16)


def block_gradients(tokens, cotangent, modulation, biases, rows_full, down_full, silu_cond):
    latents, positions, width = tokens.shape
    count, hidden_width = latents * positions, down_full.shape[0]
    own_rows = width // 4
    bf16, f32 = jnp.bfloat16, jnp.float32
    vmem = pl.BlockSpec(memory_space=pltpu.VMEM)
    return pl.pallas_call(
        block_kernel,
        out_shape=(
            jax.ShapeDtypeStruct(tokens.shape, bf16),
            jax.ShapeDtypeStruct(tokens.shape, bf16),
            jax.ShapeDtypeStruct((4, 8 * own_rows + hidden_width // 4, width), bf16),
            jax.ShapeDtypeStruct((32, width), bf16),
        ),
        in_specs=[vmem] * 7,
        out_specs=(vmem,) * 4,
        scratch_shapes=[
            pltpu.VMEM((32, width), f32),
            pltpu.VMEM((count, width), bf16),
            pltpu.VMEM((count, 3 * width), bf16),
            pltpu.VMEM((latents * HEADS, positions, positions), f32),
            pltpu.VMEM((count, width), bf16),
            pltpu.VMEM((count, width), bf16),
            pltpu.VMEM((count, hidden_width), bf16),
            pltpu.VMEM((count, hidden_width), bf16),
            pltpu.VMEM((count, width), bf16),
            pltpu.VMEM((count, width), bf16),
            pltpu.VMEM((count, width), f32),
            pltpu.VMEM((count, width), bf16),
            pltpu.VMEM((count, 3 * width), bf16),
        ],
        compiler_params=pltpu.CompilerParams(vmem_limit_bytes=VMEM_BYTES),
        name="block_gradients",
    )(tokens, cotangent, modulation, biases, rows_full, down_full, silu_cond)


def reduce_gradients(
    packed, small, w_rows, latents
):
    width = packed.shape[-1]
    own_rows, six_width = w_rows.shape[0], 6 * width
    delta_modulation = small[: 6 * latents].reshape(latents, six_width)
    silu_cond = small[6 * latents : 7 * latents]
    bias_local = small[16:24].astype(jnp.float32).reshape(-1)
    summed = lax.psum_scatter(
        packed.reshape(-1, width).astype(jnp.float32), "shard", scatter_dimension=0, tiled=True
    )
    summed = lax.psum(summed, "replica")
    axes = ("shard", "replica")
    cond_matrix = lax.all_gather(w_rows[:, :six_width], "shard", axis=0, tiled=True)
    return (
        summed,
        lax.all_gather(delta_modulation, axes, axis=0, tiled=True),
        lax.all_gather(silu_cond, axes, axis=0, tiled=True),
        lax.psum(bias_local, axes),
        matrix_multiply("le,de->ld", delta_modulation, cond_matrix),
    )


def fused_gradients(
    tokens, cotangent, modulation, biases, rows_full, down_full, silu_cond, w_rows,
    shards, replicas,
):
    latents, positions, width = tokens.shape
    count, hidden_width = latents * positions, down_full.shape[0]
    own_rows, six_width = w_rows.shape[0], 6 * width
    whole = 8 * own_rows + hidden_width // 4
    bf16, f32 = jnp.bfloat16, jnp.float32
    vmem = pl.BlockSpec(memory_space=pltpu.VMEM)
    block_out, tokens_grad, summed, every, silu_parts = pl.pallas_call(
        fused_kernel,
        out_shape=(
            jax.ShapeDtypeStruct(tokens.shape, bf16),
            jax.ShapeDtypeStruct(tokens.shape, bf16),
            jax.ShapeDtypeStruct((whole, width), bf16),
            jax.ShapeDtypeStruct((shards, 2, 4, 32, width), bf16),
            jax.ShapeDtypeStruct((shards, 16, 128), f32),
        ),
        in_specs=[vmem] * 8,
        out_specs=(vmem,) * 5,
        scratch_shapes=[
            pltpu.VMEM((32, width), f32),
            pltpu.VMEM((count, width), bf16),
            pltpu.VMEM((count, 3 * width), bf16),
            pltpu.VMEM((latents * HEADS, positions, positions), f32),
            pltpu.VMEM((count, width), bf16),
            pltpu.VMEM((count, width), bf16),
            pltpu.VMEM((count, hidden_width), bf16),
            pltpu.VMEM((count, hidden_width), bf16),
            pltpu.VMEM((count, width), bf16),
            pltpu.VMEM((count, width), bf16),
            pltpu.VMEM((count, width), f32),
            pltpu.VMEM((count, width), bf16),
            pltpu.VMEM((count, 3 * width), bf16),
            pltpu.VMEM((shards, whole, width), bf16),
            pltpu.VMEM((32, width), bf16),
            pltpu.VMEM((2, whole, width), bf16),
            pltpu.VMEM((2, whole, width), bf16),
            pltpu.VMEM((whole, width), bf16),
            pltpu.VMEM((whole, width), bf16),
            pltpu.VMEM((whole, width), bf16),
            pltpu.VMEM((whole, width), bf16),
            pltpu.VMEM((3, whole, width), bf16),
            pltpu.VMEM((shards, 16, 128), f32),
            pltpu.SemaphoreType.DMA((96,)),
            pltpu.SemaphoreType.DMA((96,)),
        ],
        compiler_params=pltpu.CompilerParams(
            collective_id=1, has_side_effects=True, vmem_limit_bytes=VMEM_BYTES
        ),
        name="fused_gradients",
    )(tokens, cotangent, modulation, biases, rows_full, down_full, silu_cond, w_rows)
    every = every.transpose(0, 2, 1, 3, 4).reshape(shards * replicas, 32, width)
    bias_rows = every[:, 16 : 16 + 8]
    delta_silu = silu_parts[:, : 6 * latents, :own_rows]
    delta_silu = delta_silu.reshape(shards, latents, 6, own_rows).sum(axis=2)
    return (
        block_out,
        tokens_grad,
        summed,
        every[:, : 6 * latents].reshape(-1, six_width),
        every[:, 6 * latents : 7 * latents].reshape(-1, width),
        bias_rows.astype(jnp.float32).sum(axis=0).reshape(-1),
        delta_silu.transpose(1, 0, 2).reshape(latents, width),
    )


def per_device(
    shards,
    replicas,
    tokens,
    condition,
    cotangent,
    w_rows,
    w_down,
    bias_pack,
    rows_first,
    rows_second,
    down_first,
    down_second,
    bias_first,
    bias_second,
):
    latents, positions, embedding_width = tokens.shape
    six_width = 6 * embedding_width
    cond_values = condition.astype(jnp.float32)
    silu_cond = jax.nn.silu(cond_values).astype(jnp.bfloat16)
    rows_full, shrink_weight, bias_full, modulation = gather_weights(
        w_rows, w_down, bias_pack, silu_cond, shards, replicas
    )
    bias_entries = bias_full.astype(jnp.float32)
    modulation = modulation + bias_entries[:six_width]
    modulation = jnp.pad(
        modulation.reshape(latents, 6, embedding_width), ((0, 0), (0, 2), (0, 0))
    )
    arguments = (
        tokens,
        cotangent,
        modulation,
        bias_entries[six_width:].reshape(-1, embedding_width),
        rows_full,
        shrink_weight,
        silu_cond,
    )
    if shards != 4 or replicas != 8 or latents != 2:
        block_out, tokens_grad, packed, small = block_gradients(*arguments)
        reduced = reduce_gradients(packed, small, w_rows, latents)
    else:
        block_out, tokens_grad, *reduced = fused_gradients(*arguments, w_rows, shards, replicas)
    summed, every_modulation, every_silu, bias_rest, delta_silu = reduced
    blocks = rows_full.shape[1] // embedding_width
    shard_rows = w_rows.shape[0]
    shard_at = lax.axis_index("shard")
    own_silu = lax.dynamic_slice_in_dim(every_silu, shard_at * shard_rows, shard_rows, 1)
    total_cond = matrix_multiply("ld,le->de", own_silu, every_modulation)
    bias_cond = jnp.sum(every_modulation.astype(jnp.float32), axis=0)
    cond_grad = jax.vjp(jax.nn.silu, cond_values)[1](delta_silu)[0]
    split_at = blocks * shard_rows
    own_rows = (
        summed[:split_at]
        .reshape(blocks, shard_rows, embedding_width)
        .transpose(1, 0, 2)
        .reshape(shard_rows, -1)
        .astype(jnp.float32)
    )
    rows_grad = jnp.concatenate([total_cond, own_rows], axis=1)
    down_grad = summed[split_at:].astype(jnp.float32)
    bias_share = bias_pack.shape[0]
    bias_grad = lax.dynamic_slice_in_dim(
        jnp.concatenate([bias_cond, bias_rest]), shard_at * bias_share, bias_share, 0
    )
    rows_new, rows_first_new, rows_second_new = adam_step(
        w_rows, rows_grad, rows_first, rows_second, decay_rate
    )
    down_new, down_first_new, down_second_new = adam_step(
        w_down, down_grad, down_first, down_second, decay_rate
    )
    bias_new, bias_first_new, bias_second_new = adam_step(
        bias_pack, bias_grad, bias_first, bias_second, 0.0
    )
    return (
        block_out,
        tokens_grad,
        cond_grad,
        rows_new,
        rows_first_new,
        rows_second_new,
        down_new,
        down_first_new,
        down_second_new,
        bias_new,
        bias_first_new,
        bias_second_new,
    )


def solution(mesh):
    placed = (
        P(("shard", "replica"), None, None),
        P(("shard", "replica"), None),
        P(("shard", "replica"), None, None),
        P("shard", None),
        P("shard", None),
        P("shard"),
        P("shard", None),
        P("shard", None),
        P("shard", None),
        P("shard", None),
        P("shard"),
        P("shard"),
    )
    return jax.shard_map(
        partial(per_device, mesh.shape["shard"], mesh.shape["replica"]),
        mesh=mesh,
        in_specs=placed,
        out_specs=(
            P(("shard", "replica"), None, None),
            P(("shard", "replica"), None, None),
            P(("shard", "replica"), None),
            P("shard", None),
            P("shard", None),
            P("shard", None),
            P("shard", None),
            P("shard", None),
            P("shard", None),
            P("shard"),
            P("shard"),
            P("shard"),
        ),
        check_vma=False,
    )
```
